32 devices in a mesh: groups: 2 (over x), node: 4 (over y, core), local: 4 (over z).
Axes of the slice: x: 2, y: 2, z: 4, core: 2. Of those that a mesh axis runs over, the one named last changes fastest.
Arguments:
- out_grad: bfloat16 [1024, 3584], P(('groups', 'node', 'local')), parts along dimension 0, may hold values from -0.29882812 to 0.29882812
- lengths: int32 [32], P('groups'), parts along dimension 0, may hold values from 1 to 64, 512 in all
- gate_weights: bfloat16 [1024, 8], P(('groups', 'node', 'local')), parts along dimension 0, may hold values from 0.049804688 to 1
- expert_ids: int32 [1024, 8], P(('groups', 'node', 'local')), parts along dimension 0, may hold values from 0 to 7, as said below
- hidden_routed: bfloat16 [8, 992, 2048], P('node', 'groups', 'local'), parts along dimension 1, may hold values from -6 to 6
- down_routed: bfloat16 [8, 2048, 3584], P('node', 'local'), may hold values from -0.125 to 0.125
- hidden_shared: bfloat16 [1024, 2048], P(('groups', 'node'), 'local'), parts along dimension 0, may hold values from -6 to 6
- down_shared: bfloat16 [2048, 3584], P('local'), may hold values from -0.125 to 0.125
Outputs:
- d_hidden_routed: bfloat16 [8, 992, 2048], P('node', 'groups', 'local'), parts along dimension 1
- d_down_routed: bfloat16 [16, 2048, 3584], P(('groups', 'node'), 'local'), parts along dimension 0
- d_gate: float32 [1024, 8], P(('groups', 'node', 'local')), parts along dimension 0
- d_hidden_shared: bfloat16 [1024, 2048], P(('groups', 'node'), 'local'), parts along dimension 0
- d_down_shared: bfloat16 [4096, 3584], P(('groups', 'local'), 'node'), parts along dimension 0
The draws below stay inside these ranges and needn't reach their ends.
There are 2 independent parts, one for each index of `groups`. The reference program is written for one: setup_inputs(seed, part) draws one part's arguments, and reference() takes and returns one part's arrays. A program takes and returns all parts, laid end to end along the dimension named above; an argument that names none is the same for every part. Nothing has to cross between parts.
Inputs may be any that keep to these rules, and one draw needn't show every extreme that they name: `expert_ids`: each token names 8 different experts; expert e belongs to node group floor(e / 2), and one token's experts lie in at most 4 node groups.
All inputs are finite; a program needn't handle non-finite values.
Results may differ from the reference program's by a relative error of at most 0.012.
Values may be sent and summed in bfloat16 or wider, within the bound.
No kernel may reach another device: no remote copies, remote signals or barrier semaphores. Data moves between devices by JAX's collectives and lax.ppermute only.
A program may use at most 128 MiB of HBM per device.

```python
import math
import jax
import jax.numpy as jnp
import numpy as np
from jax import lax

D = 3584
FF = 2048
SFF = 2048
EXPERTS_PER_NODE = 2
TOPK = 8
NODE_LIMIT = 4
LEN_MOST = 64
TOK_DEV = 32
EXPERTS = 8
TOKENS = 512
C_SRC = 31
SLOTS = 496
RESP = 16


def routing(key):
    node_score_total = EXPERTS // EXPERTS_PER_NODE
    block_total = TOKENS // TOK_DEV
    key_pop, key_node, key_hot, key_pick = jax.random.split(key, 4)
    popular = jax.random.randint(key_pop, (node_score_total,), 0, 4)
    node_ranking_score = jax.random.randint(key_node, (TOKENS, node_score_total), 0, 4096) + popular[None, :] * 1024
    favored_expert = jnp.repeat(jax.random.randint(key_hot, (block_total,), 0, EXPERTS), TOK_DEV)
    forced_choice = jnp.arange(TOKENS) % TOK_DEV <= C_SRC
    node_identifiers = jnp.arange(node_score_total)
    node_extra_score = jnp.where(forced_choice[:, None] & (node_identifiers[None, :] == (favored_expert // EXPERTS_PER_NODE)[:, None]), 1 << 20, 0)
    node_ranking_score = (node_ranking_score + node_extra_score) * node_score_total + node_identifiers[None, :]
    _, chosen = lax.top_k(node_ranking_score, NODE_LIMIT)
    candidate_total = NODE_LIMIT * EXPERTS_PER_NODE
    candidate_experts = (chosen[:, :, None] * EXPERTS_PER_NODE + jnp.arange(EXPERTS_PER_NODE)[None, None, :]).reshape(TOKENS, candidate_total)
    selection_score = jax.random.randint(key_pick, (TOKENS, candidate_total), 0, 4096)
    selection_extra = jnp.where(forced_choice[:, None] & (candidate_experts == favored_expert[:, None]), 1 << 20, 0)
    selection_score = (selection_score + selection_extra) * candidate_total + jnp.arange(candidate_total)[None, :]
    _, picked_order = lax.top_k(selection_score, TOPK)
    return jnp.take_along_axis(candidate_experts, picked_order, axis=1).astype(jnp.int32)


def draw_expert_ids(key, part):
    return routing(key)


def shard_levels(own_key, shape, cuts, least, largest):
    factor_of, own = 1.0, jax.random.fold_in(own_key, 6)
    for axis_at, blocks in cuts:
        steps = jnp.exp(jax.random.uniform(jax.random.fold_in(own, axis_at), (blocks,), jnp.float32, least / len(cuts), largest / len(cuts)))
        factor_of = factor_of * jnp.repeat(steps, shape[axis_at] // blocks).reshape([-1 if axis == axis_at else 1 for axis in range(len(shape))])
    return factor_of


def length_profile(amount, total, limit, slope):
    loads = [(1 << 20) // math.isqrt(standing ** slope) + 1 for standing in range(2, amount + 1)]
    surplus, holding = total - limit - (amount - 1), [1] * (amount - 1)
    while surplus > 0:
        candidates = [i for i in range(amount - 1) if holding[i] < limit]
        pool, budget = sum([loads[i] for i in candidates]), surplus
        for i in candidates:
            extra = min(limit - holding[i], max(1, budget * loads[i] // pool), surplus)
            holding[i] = holding[i] + extra
            surplus = surplus - extra
    return np.array([limit] + holding)


def ragged_sizes(key, amount, total, limit, lean):
    if amount == 2:
        one = jax.random.randint(key, (), max(1, total - limit), min(limit, total - 1) + 1)
        return jnp.stack([one, total - one])
    tallies = jnp.asarray(length_profile(amount, total, limit, lean), jnp.int32)
    couples = (amount - 1) // 2
    giver, taker = tallies[1:1 + 2 * couples:2], tallies[2:2 + 2 * couples:2]
    room = jnp.minimum(giver - 1, limit - taker)
    passed = jax.random.randint(jax.random.fold_in(key, 1), (couples,), 0, 1 << 20) % (room + 1)
    tallies = tallies.at[1:1 + 2 * couples:2].set(giver - passed).at[2:2 + 2 * couples:2].set(taker + passed)
    return tallies[jax.random.permutation(jax.random.fold_in(key, 2), amount)]


def gaussian(rng, extent, width, reach, pieces=(), held_as=jnp.bfloat16):
    factor_of = shard_levels(rng, extent, pieces, -0.22, 0.18) if pieces else 1.0
    values = jax.random.normal(rng, extent, jnp.float32) * width * factor_of
    return jnp.minimum(jnp.maximum(values, -reach), reach).astype(held_as)


def setup_inputs(seed: int = 0, part: int = 0) -> dict:
    keys = jax.random.split(jax.random.key(seed), 9)
    own_keys = jax.random.split(jax.random.fold_in(keys[8], part), 9)
    out_grad = gaussian(own_keys[0], (TOKENS, D), 0.05, 0.29882812, ((0, 16),))
    lengths = ragged_sizes(own_keys[1], RESP, TOKENS, LEN_MOST, 2).astype(jnp.int32)
    gate_weights = jnp.clip(jnp.exp(math.log(1.0) - 2.9996462 * jax.random.uniform(own_keys[2], (TOKENS, TOPK), jnp.float32) ** shard_levels(own_keys[2], (TOKENS, TOPK), ((0, 16),), -0.2, 0.2)), 0.049804688, 1.0).astype(jnp.bfloat16)
    expert_ids = draw_expert_ids(jax.random.fold_in(jax.random.fold_in(keys[8], part), 71), part)
    hidden_routed = gaussian(own_keys[4], (EXPERTS, SLOTS, FF), 1.0, 6.0, ((0, 4), (2, 4)))
    down_routed = gaussian(keys[5], (EXPERTS, FF, D), FF ** -0.5, 0.125, ((0, 4), (1, 4)))
    hidden_shared = gaussian(own_keys[6], (TOKENS, SFF), 1.0, 6.0, ((0, 4), (1, 4)))
    down_shared = gaussian(keys[7], (SFF, D), SFF ** -0.5, 0.125, ((0, 4),))
    return {"out_grad": out_grad, "lengths": lengths, "gate_weights": gate_weights, "expert_ids": expert_ids, "hidden_routed": hidden_routed, "down_routed": down_routed, "hidden_shared": hidden_shared, "down_shared": down_shared}


MEAN_LENGTH = 32.0


def token_weights(lengths, first, count):
    end_marks = jnp.cumsum(lengths)
    starts = end_marks - lengths
    places = first + jnp.arange(count, dtype=jnp.int32)
    inside = (places[:, None] >= starts[None, :]) & (places[:, None] < end_marks[None, :])
    own_length = jnp.sum(jnp.where(inside, lengths[None, :], 0), axis=1)
    return MEAN_LENGTH / own_length.astype(jnp.float32)


def slot_numbers(expert_ids, block, expert_total, capacity):
    token_total = expert_ids.shape[0]
    hit_count = jnp.sum((expert_ids[:, :, None] == jnp.arange(expert_total, dtype=jnp.int32)[None, None, :]).astype(jnp.int32), axis=1)
    blocked = hit_count.reshape(token_total // block, block, expert_total)
    before = (jnp.cumsum(blocked, axis=1) - blocked).reshape(token_total, expert_total).astype(jnp.int32)
    rank_value = jnp.take_along_axis(before, expert_ids, axis=1)
    return jnp.where(rank_value < capacity, rank_value, -1).astype(jnp.int32)


def per_expert(expert_items):
    expert_rows, expert_gates, hidden, weight_down = expert_items
    back_grad = jnp.dot(expert_rows, weight_down.T, preferred_element_type=jnp.float32)
    d_hidden = (expert_gates.astype(jnp.float32)[:, None] * back_grad).astype(jnp.bfloat16)
    slot_grad = jnp.sum(hidden.astype(jnp.float32) * back_grad, axis=1)
    scaled = expert_rows * expert_gates[:, None]
    grad_down = jnp.dot(hidden.T, scaled, preferred_element_type=jnp.float32).astype(jnp.bfloat16)
    return d_hidden, slot_grad, grad_down


def reference(out_grad, lengths, gate_weights, expert_ids, hidden_routed, down_routed, hidden_shared, down_shared):
    weight = token_weights(lengths, 0, TOKENS)
    grad_rows = (out_grad.astype(jnp.float32) * weight[:, None]).astype(jnp.bfloat16)
    slots = slot_numbers(expert_ids, TOK_DEV, EXPERTS, C_SRC)
    live_mask = slots >= 0
    source = (jnp.arange(TOKENS, dtype=jnp.int32) // TOK_DEV)[:, None]
    cell_index = (expert_ids * SLOTS + source * C_SRC + slots).astype(jnp.int32)
    target = jnp.where(live_mask, cell_index, EXPERTS * SLOTS).astype(jnp.int32).reshape(-1)
    all_rows = jnp.zeros((EXPERTS * SLOTS + 1, D), jnp.bfloat16).at[target].set(jnp.repeat(grad_rows, TOPK, axis=0))
    all_gates = jnp.zeros((EXPERTS * SLOTS + 1,), jnp.bfloat16).at[target].set(gate_weights.reshape(-1))
    all_rows = all_rows[:-1].reshape(EXPERTS, SLOTS, D)
    all_gates = all_gates[:-1].reshape(EXPERTS, SLOTS)
    d_hidden_routed, slot_grad, d_down_routed = lax.map(per_expert, (all_rows, all_gates, hidden_routed, down_routed))
    safe_index = jnp.where(live_mask, cell_index, 0).astype(jnp.int32)
    picked = slot_grad.reshape(-1)[safe_index]
    d_gate = jnp.where(live_mask, picked, jnp.float32(0.0))
    shared_back = jnp.dot(grad_rows, down_shared.T, preferred_element_type=jnp.float32)
    d_hidden_shared = shared_back.astype(jnp.bfloat16)
    d_down_shared = jnp.dot(hidden_shared.T, grad_rows, preferred_element_type=jnp.float32).astype(jnp.bfloat16)
    return d_hidden_routed, d_down_routed, d_gate, d_hidden_shared, d_down_shared
```

```python
import jax
import jax.numpy as jnp
from jax import lax
from jax.sharding import PartitionSpec as P

MEAN_LENGTH = 32.0
AXES = ("node", "local")
F32 = jnp.float32
BF16 = jnp.bfloat16


def dot(a, b, ca, cb):
    return lax.dot_general(a, b, (((ca,), (cb,)), ((), ())), preferred_element_type=F32)


def ring_places(node_count, local_count):
    chips = []
    for y in range(node_count // 2):
        row = range(local_count) if y % 2 == 0 else range(local_count - 1, -1, -1)
        chips += [(y, z) for z in row]
    return chips


def gather_ring(block, node_count, local_count, split):
    chips = ring_places(node_count, local_count)
    total = len(chips)

    def flat(chip, core):
        return (chip[0] * 2 + core) * local_count + chip[1]

    def shift(step):
        return [
            (flat(chips[r], c), flat(chips[(r + step) % total], c))
            for r in range(total)
            for c in (0, 1)
        ]

    swap = [(flat(chip, c), flat(chip, 1 - c)) for chip in chips for c in (0, 1)]
    up, down = shift(1), shift(-1)
    held = [(0, block)]
    forth = back = block
    for step in range(1, (total - 1) // 2 + 1):
        forth = lax.ppermute(forth, AXES, up)
        back = lax.ppermute(back, AXES, down)
        held += [(-step, forth), (step, back)]
    left = lax.ppermute(forth[:, :split], AXES, up)
    right = lax.ppermute(back[:, split:], AXES, down)
    held.append((total // 2, jnp.concatenate([left, right], axis=1)))
    node, local = lax.axis_index("node"), lax.axis_index("local")
    y, core = node // 2, node % 2
    mine = y * local_count + jnp.where(y % 2 == 0, local, local_count - 1 - local)
    blocks, offsets, cores = [], [], []
    for offset, piece in held:
        blocks += [piece, lax.ppermute(piece, AXES, swap)]
        offsets += [offset, offset]
        cores += [0, 1]
    at = (mine + jnp.array(offsets, jnp.int32) + total) % total
    at_y = at // local_count
    at_z = jnp.where(at_y % 2 == 0, at % local_count, local_count - 1 - at % local_count)
    order = (at_y * 2 + (core + jnp.array(cores, jnp.int32)) % 2) * local_count + at_z
    return blocks, order


def gather_nodes(block):
    node_count = lax.axis_size("node")
    if node_count != 4:
        return lax.all_gather(block, "node", axis=0)
    node = lax.axis_index("node")
    core_swap = [(n, n ^ 1) for n in range(4)]
    chip_swap = [(n, n ^ 2) for n in range(4)]
    across = lax.ppermute(block, "node", chip_swap)
    found = [block, lax.ppermute(block, "node", core_swap), across, lax.ppermute(across, "node", core_swap)]
    stacked = jnp.stack(found)
    return stacked[jnp.arange(4) ^ node]


def body(
    out_grad,
    lengths,
    gate_weights,
    expert_ids,
    hidden_routed,
    down_routed,
    hidden_shared,
    down_shared,
):
    node_count = lax.axis_size("node")
    local_count = lax.axis_size("local")
    device_count = node_count * local_count
    here, features = out_grad.shape
    choices = expert_ids.shape[1]
    experts, slot_total, units = hidden_routed.shape
    capacity = slot_total // device_count
    node, local = lax.axis_index("node"), lax.axis_index("local")

    pad = jnp.zeros((here, 128 - 2 * choices), BF16)
    packed = jnp.concatenate([out_grad, gate_weights, expert_ids.astype(BF16), pad], axis=1)
    if device_count <= 16:
        split = features // 2 // 128 * 128
        blocks, order = gather_ring(packed, node_count, local_count, split)
        rows = jnp.concatenate(blocks, axis=0)
    else:
        rows = lax.all_gather(packed, AXES, axis=0, tiled=True)
        order = jnp.arange(device_count, dtype=jnp.int32)
    token_total = device_count * here
    counted = jnp.arange(device_count, dtype=jnp.int32)
    place = jnp.sum(jnp.where(order[None, :] == counted[:, None], counted[None, :], 0), axis=1)

    ends = jnp.cumsum(lengths)
    places = (order[:, None] * here + jnp.arange(here, dtype=jnp.int32)[None, :]).reshape(-1)
    inside = (places[:, None] >= (ends - lengths)[None, :]) & (places[:, None] < ends[None, :])
    weight = MEAN_LENGTH / jnp.sum(jnp.where(inside, lengths[None, :], 0), axis=1).astype(F32)

    x = rows[:, :features]
    gates = rows[:, features : features + choices].astype(F32)
    ids = rows[:, features + choices : features + 2 * choices].astype(jnp.int32)
    first = node * experts
    d_hidden, d_down, sums = [], [], []
    for e in range(experts):
        named = ids == first + e
        hit = jnp.any(named, axis=1)
        gate = jnp.sum(jnp.where(named, gates, 0.0), axis=1)
        hits = hit.astype(jnp.int32).reshape(device_count, here)
        rank = (jnp.cumsum(hits, axis=1) - hits).reshape(-1)
        cell = jnp.repeat(order, here) * capacity + rank
        cell = jnp.where(hit & (rank < capacity), cell, -1)
        placing = jnp.arange(slot_total, dtype=jnp.int32)[:, None] == cell[None, :]
        placing = placing.astype(BF16)
        hidden = dot(hidden_routed[e], placing, 0, 0)
        back = dot(down_routed[e], x, 1, 1) * weight[None, :]
        sums.append(jnp.sum(hidden * back, axis=0))
        gated = placing * gate.astype(BF16)[None, :]
        d_hidden.append(dot(gated, back.astype(BF16), 1, 1).astype(BF16))
        scaled = (hidden * (gate * weight)[None, :]).astype(BF16)
        d_down.append(dot(scaled, x, 1, 0).astype(BF16))
    d_hidden_routed = jnp.stack(d_hidden)
    d_down_routed = jnp.stack(d_down)

    slot_grad = jnp.stack(sums).reshape(experts, device_count, here)[:, place]
    slot_grad = slot_grad.reshape(experts, node_count, local_count, here)

    def turn(count, step):
        return [(i, (i + step) % count) for i in range(count)]

    def own(a):
        return lax.dynamic_index_in_dim(a, local, 2, keepdims=False)

    total = own(slot_grad)
    for step in range(1, local_count):
        total = total + own(lax.ppermute(slot_grad, "local", turn(local_count, step)))
    d_gate = jnp.zeros(expert_ids.shape, F32)
    for step in range(node_count):
        got = total if step == 0 else lax.ppermute(total, "node", turn(node_count, step))
        got = lax.dynamic_index_in_dim(got, node, 1, keepdims=False)
        start = (node + node_count - step) % node_count * experts
        for e in range(experts):
            d_gate = d_gate + jnp.where(expert_ids == start + e, got[e][:, None], 0.0)

    blocked = x.reshape(device_count, here, features)
    near = lax.dynamic_slice_in_dim(place, node * local_count, local_count, 0)
    near_weight = weight.reshape(device_count, here)[near].reshape(-1)
    shared_back = dot(blocked[near].reshape(-1, features), down_shared, 1, 1)
    d_hidden_shared = (shared_back * near_weight[:, None]).astype(BF16)
    columns = features // node_count
    mine = lax.dynamic_slice_in_dim(x, node * columns, columns, 1)
    shared = gather_nodes(hidden_shared).reshape(device_count, here, -1)[order]
    shared = (shared.reshape(token_total, -1).astype(F32) * weight[:, None]).astype(BF16)
    d_down_shared = dot(shared, mine, 0, 0).astype(BF16)
    return (d_hidden_routed, d_down_routed, d_gate, d_hidden_shared, d_down_shared)


def solution(mesh):
    placed = (
        P(("groups", "node", "local"), None),
        P("groups"),
        P(("groups", "node", "local"), None),
        P(("groups", "node", "local"), None),
        P("node", "groups", "local"),
        P("node", "local", None),
        P(("groups", "node"), "local"),
        P("local", None),
    )
    return jax.shard_map(
        body,
        mesh=mesh,
        in_specs=placed,
        out_specs=(
            P("node", "groups", "local"),
            P(("groups", "node"), "local", None),
            P(("groups", "node", "local"), None),
            P(("groups", "node"), "local"),
            P(("groups", "local"), "node"),
        ),
        check_vma=False,
    )
```

```python
import jax
import jax.numpy as jnp
from jax import lax
from jax.experimental import pallas as pl
from jax.experimental.pallas import tpu as pltpu
from jax.sharding import PartitionSpec as P

MEAN_LENGTH = 32.0
AXES = ("node", "local")
F32 = jnp.float32
BF16 = jnp.bfloat16


def dot(a, b, ca, cb):
    return lax.dot_general(a, b, (((ca,), (cb,)), ((), ())), preferred_element_type=F32)


def ring_places(node_count, local_count):
    chips = []
    for y in range(node_count // 2):
        row = range(local_count) if y % 2 == 0 else range(local_count - 1, -1, -1)
        chips += [(y, z) for z in row]
    return chips


def ring_offsets(total):
    offsets = [0]
    for step in range(1, (total - 1) // 2 + 1):
        offsets += [-step, step]
    return offsets + [total // 2]


def gather_ring(rows, tags, node_count, local_count, split):
    chips = ring_places(node_count, local_count)
    total = len(chips)

    def flat(chip, core):
        return (chip[0] * 2 + core) * local_count + chip[1]

    def shift(step):
        return [
            (flat(chips[r], c), flat(chips[(r + (step if c == 0 else -step)) % total], c))
            for r in range(total)
            for c in (0, 1)
        ]

    swap = [(flat(chip, c), flat(chip, 1 - c)) for chip in chips for c in (0, 1)]
    one, two = shift(1), shift(-1)

    def send(a, perm):
        return lax.ppermute(a, AXES, perm)

    def joined(a, b):
        return jnp.concatenate([a, b], axis=1)

    core = lax.axis_index("node") % 2
    first, second = send(rows, one), send(rows, two)
    tag_first, tag_second = send(tags, one), send(tags, two)
    blocks = [joined(rows, tags), joined(send(rows, swap), send(tags, swap))]
    first, second = joined(first, tag_first), joined(second, tag_second)
    for step in range(1, (total - 1) // 2 + 1):
        if step > 1:
            first, second = send(first, one), send(second, two)
        blocks += [first, send(first, swap), second, send(second, swap)]
    first, second = send(first[:, :split], one), send(second[:, split:], two)
    last = joined(first, second)
    blocks += [last, send(last, swap)]
    return blocks


def block_numbers(node, local, node_count, local_count):
    total = node_count // 2 * local_count
    y, core = node // 2, node % 2
    sign = 1 - 2 * core
    mine = y * local_count + jnp.where(y % 2 == 0, local, local_count - 1 - local)
    steps = [(0, 0), (0, 1)]
    for s in range(1, (total - 1) // 2 + 1):
        steps += [(-s, 0), (s, 1), (s, 0), (-s, 1)]
    steps += [(total // 2, 0), (total // 2, 1)]
    numbers = []
    for offset, other in steps:
        at = (mine + sign * offset + total) % total
        at_y, at_z = at // local_count, at % local_count
        at_z = jnp.where(at_y % 2 == 0, at_z, local_count - 1 - at_z)
        at_core = core + other - 2 * core * other
        numbers.append((at_y * 2 + at_core) * local_count + at_z)
    return numbers


def lengths_at(lens_ref, tokens):
    found = jnp.zeros(tokens.shape, jnp.int32)
    end = 0
    for r in range(lens_ref.shape[0]):
        found = jnp.where(tokens >= end, lens_ref[r], found)
        end = end + lens_ref[r]
    return found.astype(F32)


def rows_kernel(counts, first_block, choices, capacity, lens_ref, where_ref, *refs):
    count = counts[2]
    blocks, refs = refs[:count], refs[count:]
    if first_block:
        before_ref, refs = refs[0], refs[1:]
    hidden_ref, down_ref, x_ref, scaled_ref, grad_ref, info_ref, sums_ref, hidden_scr = refs
    experts, slot_total, units = hidden_ref.shape
    here = blocks[0].shape[0]
    features = x_ref.shape[1]
    tokens = count * here
    node, local = where_ref[0], where_ref[1]
    numbers = block_numbers(node, local, counts[0], counts[1])[first_block : first_block + count]
    for b in range(count):
        x_ref[b * here : (b + 1) * here, :] = blocks[b][:, :features]
    tags = jnp.concatenate([ref[:, features:] for ref in blocks], axis=0).astype(F32).T
    gates, ids = tags[:choices], tags[choices : 2 * choices]
    token = lax.broadcasted_iota(jnp.int32, (1, tokens), 1)
    number = jnp.zeros((1, tokens), jnp.int32)
    for b in range(count):
        number = jnp.where(token // here == b, numbers[b], number)
    weight = MEAN_LENGTH / lengths_at(lens_ref, number * here + token % here)
    earlier = lax.broadcasted_iota(jnp.int32, (tokens, tokens), 0)
    later = lax.broadcasted_iota(jnp.int32, (tokens, tokens), 1)
    earlier = ((earlier < later) & (earlier // here == later // here)).astype(F32).astype(BF16)
    named = [ids == (node * experts + e).astype(F32) for e in range(experts)]
    hits = [jnp.sum(n.astype(F32), axis=0, keepdims=True) for n in named]
    gate = [jnp.sum(jnp.where(n, gates, 0.0), axis=0, keepdims=True) for n in named]
    row = lax.broadcasted_iota(jnp.int32, (8, tokens), 0)
    stacked = jnp.zeros((8, tokens), F32)
    for e in range(experts):
        stacked = jnp.where(row == e, hits[e], stacked)
    ranks = dot(stacked.astype(BF16), earlier, 1, 0)
    slot = lax.broadcasted_iota(jnp.int32, (slot_total, tokens), 0).astype(F32)
    info = jnp.zeros((8, tokens), F32)
    for e in range(experts):
        rank = ranks[e : e + 1]
        live = (hits[e] > 0.5) & (rank < capacity - 0.5)
        cell = jnp.where(live, number.astype(F32) * capacity + rank, -1.0)
        info = jnp.where(row == e, cell, info)
        info = jnp.where(row == experts + e, gate[e], info)
        placing = (slot == cell).astype(F32).astype(BF16)
        hidden = dot(hidden_ref[e], placing, 0, 0)
        hidden_scr[e] = hidden.astype(BF16)
        scaled_ref[e] = (hidden * (gate[e] * weight)).astype(BF16)
    info_ref[...] = info
    step = 256 if units % 256 == 0 else units
    sums = jnp.zeros((8, tokens), F32)
    for e in range(experts):

        def part(i, total, e=e):
            at = pl.ds(pl.multiple_of(i * step, step), step)
            back = dot(down_ref[e, at, :], x_ref[...], 1, 1) * weight
            grad_ref[e, at, :] = back.astype(BF16)
            return total + jnp.sum(back * hidden_scr[e, at, :].astype(F32), axis=0, keepdims=True)

        total = lax.fori_loop(0, units // step, part, jnp.zeros((1, tokens), F32))
        sums = jnp.where(row == e, total, sums)
    if first_block:
        sums_ref[...] = before_ref[...]
    else:
        sums_ref[...] = jnp.zeros(sums_ref.shape, F32)
    for b in range(count):
        sums_ref[numbers[b]] = sums[:experts, b * here : (b + 1) * here]


VMEM = pl.BlockSpec(memory_space=pltpu.VMEM)
SMEM = pl.BlockSpec(memory_space=pltpu.SMEM)


def rows_call(counts, first_block, choices, capacity, lengths, where, blocks, before, hidden, down):
    count = len(blocks)
    here = blocks[0].shape[0]
    experts, _, units = hidden.shape
    features = down.shape[2]
    tokens = count * here
    device_count = counts[0] * counts[1]
    given = [lengths, where, *blocks] + ([before] if first_block else []) + [hidden, down]
    return pl.pallas_call(
        lambda *refs: rows_kernel((*counts, count), first_block, choices, capacity, *refs),
        out_shape=(
            jax.ShapeDtypeStruct((tokens, features), BF16),
            jax.ShapeDtypeStruct((experts, units, tokens), BF16),
            jax.ShapeDtypeStruct((experts, units, tokens), BF16),
            jax.ShapeDtypeStruct((8, tokens), F32),
            jax.ShapeDtypeStruct((device_count, experts, here), F32),
        ),
        in_specs=[SMEM, SMEM] + [VMEM] * (len(given) - 2),
        out_specs=[VMEM] * 5,
        scratch_shapes=[pltpu.VMEM((experts, units, tokens), BF16)],
        compiler_params=pltpu.CompilerParams(vmem_limit_bytes=16 * 2**20),
        cost_estimate=pl.CostEstimate(
            flops=2 * tokens * experts * units * features,
            bytes_accessed=2 * experts * units * features,
            transcendentals=0,
        ),
        name="rows_first" if not first_block else "rows_second",
    )(*given)


def weights_kernel(
    counts,
    tile,
    lens_ref,
    where_ref,
    x_a,
    x_b,
    scaled_a,
    scaled_b,
    grad_a,
    grad_b,
    info_a,
    info_b,
    shared_0,
    shared_1,
    shared_2,
    shared_3,
    down_ref,
    d_down_ref,
    d_hidden_ref,
    d_hidden_shared_ref,
    d_down_shared_ref,
    shared_scr,
    ordered_scr,
    near_scr,
):
    experts = scaled_a.shape[0]
    tokens, features = x_a.shape
    slot_total = d_hidden_ref.shape[1]
    node_tokens = shared_0.shape[0]
    node_count, local_count = counts
    here = node_tokens // local_count
    node, local = where_ref[0], where_ref[1]
    i = pl.program_id(0)
    at = pl.ds(pl.multiple_of(i * tile, tile), tile)
    for e in range(experts):
        total = dot(scaled_a[e], x_a[:, at], 1, 0) + dot(scaled_b[e], x_b[:, at], 1, 0)
        d_down_ref[e] = total.astype(BF16)

    for e in range(experts):

        @pl.when(i == 1 + e)
        def _(e=e):
            slot = lax.broadcasted_iota(jnp.int32, (slot_total, tokens), 0).astype(F32)
            total = jnp.zeros((slot_total, grad_a.shape[1]), F32)
            for info, grad in ((info_a, grad_a), (info_b, grad_b)):
                gate = info[experts + e : experts + e + 1, :]
                gated = jnp.where(slot == info[e : e + 1, :], gate, 0.0).astype(BF16)
                total = total + dot(gated, grad[e], 1, 1)
            d_hidden_ref[e] = total.astype(BF16)

    @pl.when(i == 1 + experts)
    def _():
        numbers = block_numbers(node, local, node_count, local_count)
        half = len(numbers) // 2
        for b, number in enumerate(numbers):
            x = x_a if b < half else x_b
            rows = x.at[(b % half) * here : (b % half + 1) * here, :]

            @pl.when(number // local_count == node)
            def _(rows=rows, number=number):
                to = pl.ds(pl.multiple_of(number % local_count * here, here), here)
                near_scr[to, :] = rows[...]

        spread = lax.broadcasted_iota(jnp.int32, (node_tokens, 128), 0)
        weight = MEAN_LENGTH / lengths_at(lens_ref, node * node_tokens + spread)[:, :1]
        back = dot(near_scr[...], down_ref[...], 1, 1)
        d_hidden_shared_ref[...] = (back * weight).astype(BF16)

    @pl.when(i == 2 + experts)
    def _():
        spread = lax.broadcasted_iota(jnp.int32, (node_tokens, 128), 0)
        for step, shared in enumerate((shared_0, shared_1, shared_2, shared_3)):
            n = node + step - 2 * (node & step)
            weight = MEAN_LENGTH / lengths_at(lens_ref, n * node_tokens + spread)[:, :1]
            to = pl.ds(pl.multiple_of(n * node_tokens, node_tokens), node_tokens)
            shared_scr[to, :] = (shared[...].astype(F32) * weight).astype(BF16)
        numbers = block_numbers(node, local, node_count, local_count)
        for b, number in enumerate(numbers):
            rows = pl.ds(pl.multiple_of(number * here, here), here)
            ordered_scr[b * here : (b + 1) * here, :] = shared_scr[rows, :]
        width = d_down_shared_ref.shape[1]
        columns = pl.ds(pl.multiple_of(node * width, width), width)
        total = dot(ordered_scr[:tokens, :], x_a[:, columns], 0, 0)
        total = total + dot(ordered_scr[tokens:, :], x_b[:, columns], 0, 0)
        d_down_shared_ref[...] = total.astype(BF16)


def weights_call(counts, slot_total, lengths, where, first, second, shared, down_shared):
    x_a, scaled_a, grad_a, info_a, _ = first
    x_b, scaled_b, grad_b, info_b, _ = second
    experts, units, tokens = scaled_a.shape
    features = x_a.shape[1]
    node_tokens, shared_units = shared[0].shape
    tile = 512 if features % 512 == 0 else 128
    width = features // counts[0]
    whole = lambda *shape: pl.BlockSpec(shape, lambda i: (0,) * len(shape))
    return pl.pallas_call(
        lambda *refs: weights_kernel(counts, tile, *refs),
        grid=(features // tile,),
        out_shape=(
            jax.ShapeDtypeStruct((experts, units, features), BF16),
            jax.ShapeDtypeStruct((experts, slot_total, units), BF16),
            jax.ShapeDtypeStruct((node_tokens, shared_units), BF16),
            jax.ShapeDtypeStruct((shared_units, width), BF16),
        ),
        in_specs=[SMEM, SMEM] + [VMEM] * 13,
        out_specs=(
            pl.BlockSpec((experts, units, tile), lambda i: (0, 0, i)),
            whole(experts, slot_total, units),
            whole(node_tokens, shared_units),
            whole(shared_units, width),
        ),
        scratch_shapes=[
            pltpu.VMEM((4 * node_tokens, shared_units), BF16),
            pltpu.VMEM((4 * node_tokens, shared_units), BF16),
            pltpu.VMEM((node_tokens, features), BF16),
        ],
        compiler_params=pltpu.CompilerParams(vmem_limit_bytes=20 * 2**20),
        cost_estimate=pl.CostEstimate(
            flops=4 * tokens * experts * units * features,
            bytes_accessed=2 * experts * units * features,
            transcendentals=0,
        ),
        name="weights",
    )(lengths, where, x_a, x_b, scaled_a, scaled_b, grad_a, grad_b, info_a, info_b, *shared, down_shared)


def swapped_nodes(block):
    core_swap = [(n, n ^ 1) for n in range(4)]
    chip_swap = [(n, n ^ 2) for n in range(4)]
    across = lax.ppermute(block, "node", chip_swap)
    return [block, lax.ppermute(block, "node", core_swap), across, lax.ppermute(across, "node", core_swap)]


def return_gates(slot_grad, expert_ids, experts):
    node_count, local_count = lax.axis_size("node"), lax.axis_size("local")
    node, local = lax.axis_index("node"), lax.axis_index("local")
    here = expert_ids.shape[0]
    slot_grad = slot_grad.reshape(node_count, local_count, experts, here)

    def turn(count, step):
        return [(i, (i + step) % count) for i in range(count)]

    def own(a):
        return lax.dynamic_index_in_dim(a, local, 1, keepdims=False)

    total = own(slot_grad)
    for step in range(1, local_count):
        total = total + own(lax.ppermute(slot_grad, "local", turn(local_count, step)))
    d_gate = jnp.zeros(expert_ids.shape, F32)
    for step in range(node_count):
        got = total if step == 0 else lax.ppermute(total, "node", turn(node_count, step))
        got = lax.dynamic_index_in_dim(got, node, 0, keepdims=False)
        start = (node + node_count - step) % node_count * experts
        for e in range(experts):
            d_gate = d_gate + jnp.where(expert_ids == start + e, got[e][:, None], 0.0)
    return d_gate


def wide_body(
    out_grad,
    lengths,
    gate_weights,
    expert_ids,
    hidden_routed,
    down_routed,
    hidden_shared,
    down_shared,
):
    node_count = lax.axis_size("node")
    local_count = lax.axis_size("local")
    device_count = node_count * local_count
    here, features = out_grad.shape
    choices = expert_ids.shape[1]
    experts, slot_total, units = hidden_routed.shape
    capacity = slot_total // device_count
    node = lax.axis_index("node")
    pad = jnp.zeros((here, 128 - 2 * choices), BF16)
    packed = jnp.concatenate([out_grad, gate_weights, expert_ids.astype(BF16), pad], axis=1)
    rows = lax.all_gather(packed, AXES, axis=0, tiled=True)
    token_total = device_count * here
    ends = jnp.cumsum(lengths)
    places = jnp.arange(token_total, dtype=jnp.int32)
    inside = (places[:, None] >= (ends - lengths)[None, :]) & (places[:, None] < ends[None, :])
    weight = MEAN_LENGTH / jnp.sum(jnp.where(inside, lengths[None, :], 0), axis=1).astype(F32)
    x = rows[:, :features]
    gates = rows[:, features : features + choices].astype(F32)
    ids = rows[:, features + choices : features + 2 * choices].astype(jnp.int32)
    d_hidden, d_down, sums = [], [], []
    for e in range(experts):
        named = ids == node * experts + e
        hit = jnp.any(named, axis=1)
        gate = jnp.sum(jnp.where(named, gates, 0.0), axis=1)
        hits = hit.astype(jnp.int32).reshape(device_count, here)
        rank = (jnp.cumsum(hits, axis=1) - hits).reshape(-1)
        cell = places // here * capacity + rank
        cell = jnp.where(hit & (rank < capacity), cell, -1)
        placing = jnp.arange(slot_total, dtype=jnp.int32)[:, None] == cell[None, :]
        placing = placing.astype(BF16)
        hidden = dot(hidden_routed[e], placing, 0, 0)
        back = dot(down_routed[e], x, 1, 1) * weight[None, :]
        sums.append(jnp.sum(hidden * back, axis=0))
        gated = placing * gate.astype(BF16)[None, :]
        d_hidden.append(dot(gated, back.astype(BF16), 1, 1).astype(BF16))
        scaled = (hidden * (gate * weight)[None, :]).astype(BF16)
        d_down.append(dot(scaled, x, 1, 0).astype(BF16))
    slot_grad = jnp.stack(sums).reshape(experts, device_count, here)
    d_gate = return_gates(jnp.swapaxes(slot_grad, 0, 1), expert_ids, experts)
    near_total = local_count * here
    near = lax.dynamic_slice_in_dim(x, node * near_total, near_total, 0)
    near_weight = lax.dynamic_slice_in_dim(weight, node * near_total, near_total, 0)
    shared_back = dot(near, down_shared, 1, 1)
    d_hidden_shared = (shared_back * near_weight[:, None]).astype(BF16)
    columns = features // node_count
    mine = lax.dynamic_slice_in_dim(x, node * columns, columns, 1)
    shared = lax.all_gather(hidden_shared, "node", axis=0, tiled=True)
    shared = (shared.astype(F32) * weight[:, None]).astype(BF16)
    d_down_shared = dot(shared, mine, 0, 0).astype(BF16)
    return (jnp.stack(d_hidden), jnp.stack(d_down), d_gate, d_hidden_shared, d_down_shared)


def body(
    out_grad,
    lengths,
    gate_weights,
    expert_ids,
    hidden_routed,
    down_routed,
    hidden_shared,
    down_shared,
):
    counts = lax.axis_size("node"), lax.axis_size("local")
    device_count = counts[0] * counts[1]
    here, features = out_grad.shape
    choices = expert_ids.shape[1]
    experts, slot_total, units = hidden_routed.shape
    capacity = slot_total // device_count
    where = jnp.stack([lax.axis_index("node"), lax.axis_index("local")]).astype(jnp.int32)
    pad = jnp.zeros((here, 128 - 2 * choices), BF16)
    tags = jnp.concatenate([gate_weights, expert_ids.astype(BF16), pad], axis=1)
    blocks = gather_ring(out_grad, tags, *counts, features // 2 // 128 * 128)
    half = len(blocks) // 2
    shared = swapped_nodes(hidden_shared)
    first = rows_call(
        counts, 0, choices, capacity, lengths, where, blocks[:half], None, hidden_routed, down_routed
    )
    second = rows_call(
        counts, half, choices, capacity, lengths, where, blocks[half:], first[4], hidden_routed, down_routed
    )
    d_gate = return_gates(second[4], expert_ids, experts)
    d_down_routed, d_hidden_routed, d_hidden_shared, d_down_shared = weights_call(
        counts, slot_total, lengths, where, first, second, shared, down_shared
    )
    return (d_hidden_routed, d_down_routed, d_gate, d_hidden_shared, d_down_shared)


def solution(mesh):
    placed = (
        P(("groups", "node", "local"), None),
        P("groups"),
        P(("groups", "node", "local"), None),
        P(("groups", "node", "local"), None),
        P("node", "groups", "local"),
        P("node", "local", None),
        P(("groups", "node"), "local"),
        P("local", None),
    )
    small = mesh.shape["node"] == 4 and mesh.shape["local"] == 4
    return jax.shard_map(
        body if small else wide_body,
        mesh=mesh,
        in_specs=placed,
        out_specs=(
            P("node", "groups", "local"),
            P(("groups", "node"), "local", None),
            P(("groups", "node", "local"), None),
            P(("groups", "node"), "local"),
            P(("groups", "local"), "node"),
        ),
        check_vma=False,
    )
```

```python
import jax
import jax.numpy as jnp
from jax import lax
from jax.experimental import pallas as pl
from jax.experimental.pallas import tpu as pltpu
from jax.sharding import PartitionSpec as P

MEAN_LENGTH = 32.0
AXES = ("node", "local")
F32 = jnp.float32
BF16 = jnp.bfloat16


def dot(a, b, ca, cb):
    return lax.dot_general(a, b, (((ca,), (cb,)), ((), ())), preferred_element_type=F32)


def ring_places(node_count, local_count):
    chips = []
    for y in range(node_count // 2):
        row = range(local_count) if y % 2 == 0 else range(local_count - 1, -1, -1)
        chips += [(y, z) for z in row]
    return chips


def ring_shift(node_count, local_count, step):
    chips = ring_places(node_count, local_count)
    pairs = []
    for r, chip in enumerate(chips):
        to = chips[(r + step) % len(chips)]
        for core in (0, 1):
            pairs.append(
                ((chip[0] * 2 + core) * local_count + chip[1], (to[0] * 2 + core) * local_count + to[1])
            )
    return pairs


def block_numbers(node, local, node_count, local_count):
    total = node_count // 2 * local_count
    y, core = node // 2, node % 2
    mine = y * local_count + jnp.where(y % 2 == 0, local, local_count - 1 - local)
    offsets = [0]
    for step in range(1, (total - 1) // 2 + 1):
        offsets += [-step, step]
    offsets.append(total // 2)
    numbers = []
    for offset in offsets:
        at = (mine + offset + total) % total
        at_y, at_z = at // local_count, at % local_count
        at_z = jnp.where(at_y % 2 == 0, at_z, local_count - 1 - at_z)
        for at_core in (core, 1 - core):
            numbers.append((at_y * 2 + at_core) * local_count + at_z)
    return numbers


def lengths_at(lens_ref, tokens):
    found = jnp.zeros(tokens.shape, jnp.int32)
    end = 0
    for r in range(lens_ref.shape[0]):
        found = jnp.where(tokens >= end, lens_ref[r], found)
        end = end + lens_ref[r]
    return found.astype(F32)


VMEM = pl.BlockSpec(memory_space=pltpu.VMEM)
SMEM = pl.BlockSpec(memory_space=pltpu.SMEM)
ANY = pl.BlockSpec(memory_space=pl.ANY)
MIB = 2**20
WEIGHTS_FLOPS = 20 * 10**9
HALF_FLOPS = 6 * 10**9
SHARED_FLOPS = 3 * 10**9
PACK_MIB = 50
LAST_MIB = 40
ROWS_BYTES = 66 * MIB
LITTLE = pl.CostEstimate(flops=10**6, bytes_accessed=10**4, transcendentals=0)


def numbers_at(numbers, tokens, here):
    token = lax.broadcasted_iota(jnp.int32, (1, tokens), 1)
    found = jnp.zeros((1, tokens), jnp.int32)
    for b, number in enumerate(numbers):
        found = jnp.where(token >= b * here, number, found)
    return found


def pack_call(out_grad, gates, ids):
    here, features = out_grad.shape
    choices = gates.shape[0]

    def kernel(rows_ref, gates_ref, ids_ref, out_ref, gates_scr, ids_scr, sems):
        pairs = ((gates_ref, gates_scr), (ids_ref, ids_scr), (rows_ref, out_ref.at[:, :features]))
        copies = [pltpu.make_async_copy(a, b, sems.at[n]) for n, (a, b) in enumerate(pairs)]
        for copy in copies:
            copy.start()
        for copy in copies[:2]:
            copy.wait()
        pad = jnp.zeros((128 - 2 * choices, here), F32)
        tags = jnp.concatenate([gates_scr[...].astype(F32), ids_scr[...].astype(F32), pad], axis=0)
        out_ref[:, features:] = tags.T.astype(BF16)
        copies[2].wait()

    return pl.pallas_call(
        kernel,
        out_shape=jax.ShapeDtypeStruct((here, features + 128), BF16),
        in_specs=[ANY] * 3,
        out_specs=VMEM,
        scratch_shapes=[
            pltpu.VMEM(gates.shape, gates.dtype),
            pltpu.VMEM(ids.shape, ids.dtype),
            pltpu.SemaphoreType.DMA((3,)),
        ],
        compiler_params=pltpu.CompilerParams(vmem_limit_bytes=PACK_MIB * MIB),
        cost_estimate=LITTLE,
        name="pack",
    )(out_grad, gates, ids)


def weights_call(counts, lengths, where, shared):
    node_tokens, _ = shared.shape
    here = node_tokens // counts[1]
    tokens = counts[0] * node_tokens

    def kernel(lens_ref, where_ref, shared_ref, weight_ref, out_ref):
        node, local = where_ref[0], where_ref[1]
        number = numbers_at(block_numbers(node, local, *counts), tokens, here)
        token = lax.broadcasted_iota(jnp.int32, (1, tokens), 1)
        row = lax.broadcasted_iota(jnp.int32, (8, tokens), 0)
        weight = MEAN_LENGTH / lengths_at(lens_ref, number * here + token % here)
        near = MEAN_LENGTH / lengths_at(lens_ref, node * node_tokens + token % node_tokens)
        weight_ref[...] = jnp.where(row == 0, weight, near)
        spread = lax.broadcasted_iota(jnp.int32, (node_tokens, 128), 0)
        column = MEAN_LENGTH / lengths_at(lens_ref, node * node_tokens + spread)[:, :1]
        out_ref[...] = (shared_ref[...].astype(F32) * column).astype(BF16)

    return pl.pallas_call(
        kernel,
        out_shape=(jax.ShapeDtypeStruct((8, tokens), F32), jax.ShapeDtypeStruct(shared.shape, BF16)),
        in_specs=[SMEM, SMEM, VMEM],
        out_specs=[VMEM] * 2,
        compiler_params=pltpu.CompilerParams(vmem_limit_bytes=4 * MIB),
        cost_estimate=pl.CostEstimate(flops=WEIGHTS_FLOPS, bytes_accessed=10**6, transcendentals=0),
        name="weights",
    )(lengths, where, shared)


def place(node, numbers, capacity, blocks, weight, hidden_ref, features, choices):
    here = blocks[0].shape[0]
    tokens = here * len(blocks)
    experts, slot_total, _ = hidden_ref.shape
    tags = jnp.concatenate([block[:, features:] for block in blocks], axis=0).astype(F32).T
    gates, ids = tags[:choices], tags[choices : 2 * choices]
    number = numbers_at(numbers, tokens, here).astype(F32)
    token = lax.broadcasted_iota(jnp.int32, (1, tokens), 1)
    first = token - token % here
    down = lax.broadcasted_iota(jnp.int32, (tokens, 1), 0)
    earlier = ((down < token) & (down >= first)).astype(F32).astype(BF16)
    named = [ids == (node * experts + e).astype(F32) for e in range(experts)]
    hits = [jnp.sum(n.astype(F32), axis=0, keepdims=True) for n in named]
    gate = [jnp.sum(jnp.where(n, gates, 0.0), axis=0, keepdims=True) for n in named]
    row = lax.broadcasted_iota(jnp.int32, (8, tokens), 0)
    stacked = jnp.zeros((8, tokens), F32)
    for e in range(experts):
        stacked = jnp.where(row == e, hits[e], stacked)
    ranks = dot(stacked.astype(BF16), earlier, 1, 0)
    slot = lax.broadcasted_iota(jnp.int32, (slot_total, 1), 0).astype(F32)
    info = jnp.zeros((8, tokens), F32)
    placed, scaled = [], []
    for e in range(experts):
        rank = ranks[e : e + 1]
        live = (hits[e] > 0.5) & (rank < capacity - 0.5)
        cell = jnp.where(live, number * capacity + rank, -1.0)
        info = jnp.where(row == e, cell, info)
        info = jnp.where(row == experts + e, gate[e], info)
        placing = (slot == cell).astype(F32).astype(BF16)
        hidden = dot(hidden_ref[e], placing, 0, 0)
        placed.append(hidden.astype(BF16))
        scaled.append((hidden * (gate[e] * weight)).astype(BF16))
    return info, placed, scaled


def half_call(counts, capacity, choices, start, where, weights, blocks, down, hidden, rows, sums):
    experts, units, features = down.shape
    count, here = len(blocks), blocks[0].shape[0]
    tokens = here * count
    device_count = counts[0] * counts[1]
    first = start * here
    step = 256 if units % 256 == 0 else units
    more = [] if rows is None else [rows, sums]

    def kernel(where_ref, *refs):
        blocks, (weights_ref, down_ref, hidden_ref), refs = refs[:count], refs[count : count + 3], refs[count + 3 :]
        before, refs = refs[: len(more)], refs[len(more) :]
        rows_ref, grad_ref, scaled_ref, info_ref, sums_ref, x_scr, grad_scr, scaled_scr, placed_scr, sems = refs
        copies = []

        def write(scr, ref):
            copies.append(pltpu.make_async_copy(scr, ref, sems.at[len(copies)]))
            copies[-1].start()

        node, local = where_ref[0], where_ref[1]
        numbers = block_numbers(node, local, *counts)[start : start + count]
        for b, block in enumerate(blocks):
            x_scr[b * here : (b + 1) * here, :] = block[:, :features]
        write(x_scr, rows_ref.at[pl.ds(first, tokens)])
        weight = weights_ref[:1, first : first + tokens]
        info, placed, scaled = place(node, numbers, capacity, blocks, weight, hidden_ref, features, choices)
        info_ref[...] = info
        for e in range(experts):
            scaled_scr[e] = scaled[e]
            placed_scr[e] = placed[e]
        write(scaled_scr, scaled_ref)
        row = lax.broadcasted_iota(jnp.int32, (8, tokens), 0)
        total = jnp.zeros((8, tokens), F32)
        for e in range(experts):
            for i in range(0, units, step):
                at = slice(i, i + step)
                back = dot(down_ref[e, at, :], x_scr[...], 1, 1) * weight
                grad_scr[e, at, :] = back.astype(BF16)
                found = jnp.sum(back * placed_scr[e, at, :].astype(F32), axis=0, keepdims=True)
                total = total + jnp.where(row == e, found, 0.0)
            write(grad_scr.at[e], grad_ref.at[e])
        if more:
            sums_ref[...] = before[1][...]
        else:
            sums_ref[...] = jnp.zeros(sums_ref.shape, F32)
        for b, number in enumerate(numbers):
            sums_ref[number] = total[:experts, b * here : (b + 1) * here]
        for copy in copies:
            copy.wait()

    return pl.pallas_call(
        kernel,
        out_shape=(
            jax.ShapeDtypeStruct((-(-ROWS_BYTES // (2 * features)), features), BF16),
            jax.ShapeDtypeStruct((experts, units, tokens), BF16),
            jax.ShapeDtypeStruct((experts, units, tokens), BF16),
            jax.ShapeDtypeStruct((8, tokens), F32),
            jax.ShapeDtypeStruct((device_count, experts, here), F32),
        ),
        in_specs=[SMEM] + [VMEM] * (count + 3) + [ANY, VMEM][: len(more)],
        out_specs=[ANY, ANY, ANY, VMEM, VMEM],
        input_output_aliases={count + 4: 0} if more else {},
        scratch_shapes=[
            pltpu.VMEM((tokens, features), BF16),
            pltpu.VMEM((experts, units, tokens), BF16),
            pltpu.VMEM((experts, units, tokens), BF16),
            pltpu.VMEM((experts, units, tokens), BF16),
            pltpu.SemaphoreType.DMA((2 + experts,)),
        ],
        compiler_params=pltpu.CompilerParams(vmem_limit_bytes=12 * MIB),
        cost_estimate=pl.CostEstimate(flops=HALF_FLOPS, bytes_accessed=10**6, transcendentals=0),
        name="half_second" if more else "half_first",
    )(where, *blocks, weights, down, hidden, *more)


def last_call(counts, slot_total, where, rows, first, second, shared):
    experts, units, tokens = first[1].shape
    features = rows.shape[1]
    node_tokens, shared_units = shared[0].shape
    width = features // counts[0]
    here = node_tokens // counts[1]
    step = 256 if units % 256 == 0 else units
    parts = units // step

    def kernel(where_ref, rows_ref, *refs):
        given, (info_a, info_b), shared, refs = refs[:4], refs[4:6], refs[6:10], refs[10:]
        down_ref, hidden_ref, shared_ref = refs[:3]
        x_scr, grad_scr, scaled_scr, all_scr, ordered_scr, down_scr, hidden_scr, shared_scr, sems, out_sems = refs[3:]
        loads, copies = [], []

        def load(ref, scr):
            loads.append(pltpu.make_async_copy(ref, scr, sems.at[len(loads)]))
            loads[-1].start()

        def write(scr, ref):
            copies.append(pltpu.make_async_copy(scr, ref, out_sems.at[len(copies)]))
            copies[-1].start()

        for ref, scr in zip(given, (grad_scr, grad_scr, scaled_scr, scaled_scr)):
            load(ref, scr.at[:, :, pl.ds(len(loads) % 2 * tokens, tokens)])
        load(rows_ref.at[pl.ds(0, 2 * tokens)], x_scr)
        node, local = where_ref[0], where_ref[1]
        for n, part in enumerate(shared):
            at = pl.multiple_of((node ^ n) * node_tokens, node_tokens)
            all_scr[pl.ds(at, node_tokens), :] = part[...]
        for b, number in enumerate(block_numbers(node, local, *counts)):
            of = pl.ds(pl.multiple_of(number * here, here), here)
            ordered_scr[b * here : (b + 1) * here, :] = all_scr[of, :]
        slot = lax.broadcasted_iota(jnp.int32, (slot_total, 1), 0).astype(F32)

        def by_slot(e):
            gated = []
            for info in (info_a, info_b):
                gate = info[experts + e : experts + e + 1, :]
                gated.append(jnp.where(slot == info[e : e + 1, :], gate, 0.0).astype(BF16))
            hidden_scr[e] = dot(jnp.concatenate(gated, axis=1), grad_scr[e], 1, 1).astype(BF16)
            write(hidden_scr.at[e], hidden_ref.at[e])

        for copy in loads[:2]:
            copy.wait()
        for e in range(experts - 1):
            by_slot(e)
        for copy in loads[2:]:
            copy.wait()
        for e in range(experts):
            for n in range(parts):
                at = slice(n * step, (n + 1) * step)
                place = down_scr.at[e * parts + n]
                place[...] = dot(scaled_scr[e, at, :], x_scr[...], 1, 0).astype(BF16)
                write(place, down_ref.at[e, pl.ds(n * step, step)])
        columns = pl.ds(pl.multiple_of(node * width, width), width)
        shared_scr[...] = dot(ordered_scr[...], x_scr[:, columns], 0, 0).astype(BF16)
        write(shared_scr, shared_ref)
        by_slot(experts - 1)
        for copy in copies:
            copy.wait()

    return pl.pallas_call(
        kernel,
        out_shape=(
            jax.ShapeDtypeStruct((experts, units, features), BF16),
            jax.ShapeDtypeStruct((experts, slot_total, units), BF16),
            jax.ShapeDtypeStruct((shared_units, width), BF16),
        ),
        in_specs=[SMEM] + [ANY] * 5 + [VMEM] * 6,
        out_specs=[ANY] * 3,
        scratch_shapes=[
            pltpu.VMEM((2 * tokens, features), BF16),
            pltpu.VMEM((experts, units, 2 * tokens), BF16),
            pltpu.VMEM((experts, units, 2 * tokens), BF16),
            pltpu.VMEM((4 * node_tokens, shared_units), BF16),
            pltpu.VMEM((4 * node_tokens, shared_units), BF16),
            pltpu.VMEM((experts * parts, step, features), BF16),
            pltpu.VMEM((experts, slot_total, units), BF16),
            pltpu.VMEM((shared_units, width), BF16),
            pltpu.SemaphoreType.DMA((5,)),
            pltpu.SemaphoreType.DMA((experts * parts + experts + 1,)),
        ],
        compiler_params=pltpu.CompilerParams(vmem_limit_bytes=LAST_MIB * MIB),
        cost_estimate=pl.CostEstimate(flops=8 * 10**9, bytes_accessed=10**7, transcendentals=0),
        name="last",
    )(where, rows, first[1], second[1], first[2], second[2], first[3], second[3], *shared)


def shared_back_call(counts, where, weights, blocks, down):
    units, features = down.shape
    here = blocks[0].shape[0]
    tokens = here * counts[1]

    def kernel(where_ref, *refs):
        blocks, (weights_ref, down_ref, out_ref, near_scr) = refs[:-4], refs[-4:]
        node, local = where_ref[0], where_ref[1]
        for block, number in zip(blocks, block_numbers(node, local, *counts)[::2]):

            @pl.when(number // counts[1] == node)
            def _(block=block, number=number):
                to = pl.ds(pl.multiple_of(number % counts[1] * here, here), here)
                near_scr[to, :] = block[:, :features]

        back = dot(down_ref[...], near_scr[...], 1, 1) * weights_ref[1:2, :tokens]
        out_ref[...] = back.T.astype(BF16)

    return pl.pallas_call(
        kernel,
        out_shape=jax.ShapeDtypeStruct((tokens, units), BF16),
        in_specs=[SMEM] + [VMEM] * (len(blocks) + 2),
        out_specs=VMEM,
        scratch_shapes=[pltpu.VMEM((tokens, features), BF16)],
        compiler_params=pltpu.CompilerParams(vmem_limit_bytes=12 * MIB),
        cost_estimate=pl.CostEstimate(flops=SHARED_FLOPS, bytes_accessed=10**6, transcendentals=0),
        name="shared_back",
    )(where, *blocks, weights, down)


def gates_call(counts, parts, ids):
    experts = parts.shape[1]

    def kernel(ids_ref, parts_ref, out_ref):
        d_gate = jnp.zeros(out_ref.shape, F32)
        for node in range(counts[0]):
            total = parts_ref[node * counts[1]]
            for local in range(1, counts[1]):
                total = total + parts_ref[node * counts[1] + local]
            for e in range(experts):
                d_gate = d_gate + jnp.where(ids_ref[...] == node * experts + e, total[e : e + 1], 0.0)
        out_ref[...] = d_gate

    return pl.pallas_call(
        kernel,
        out_shape=jax.ShapeDtypeStruct(ids.shape, F32),
        in_specs=[VMEM] * 2,
        out_specs=VMEM,
        compiler_params=pltpu.CompilerParams(vmem_limit_bytes=4 * MIB),
        cost_estimate=LITTLE,
        name="gates",
    )(ids, parts)


def exchanged(a):
    return lax.all_to_all(a, AXES, split_axis=0, concat_axis=0, tiled=True)


def wide_body(
    out_grad,
    lengths,
    gate_weights,
    expert_ids,
    hidden_routed,
    down_routed,
    hidden_shared,
    down_shared,
):
    node_count = lax.axis_size("node")
    local_count = lax.axis_size("local")
    device_count = node_count * local_count
    here, features = out_grad.shape
    choices = expert_ids.shape[1]
    experts, slot_total, units = hidden_routed.shape
    capacity = slot_total // device_count
    node = lax.axis_index("node")
    pad = jnp.zeros((here, 128 - 2 * choices), BF16)
    packed = jnp.concatenate([out_grad, gate_weights, expert_ids.astype(BF16), pad], axis=1)
    rows = lax.all_gather(packed, AXES, axis=0, tiled=True)
    token_total = device_count * here
    ends = jnp.cumsum(lengths)
    places = jnp.arange(token_total, dtype=jnp.int32)
    inside = (places[:, None] >= (ends - lengths)[None, :]) & (places[:, None] < ends[None, :])
    weight = MEAN_LENGTH / jnp.sum(jnp.where(inside, lengths[None, :], 0), axis=1).astype(F32)
    x = rows[:, :features]
    gates = rows[:, features : features + choices].astype(F32)
    ids = rows[:, features + choices : features + 2 * choices].astype(jnp.int32)
    d_hidden, d_down, sums = [], [], []
    for e in range(experts):
        named = ids == node * experts + e
        hit = jnp.any(named, axis=1)
        gate = jnp.sum(jnp.where(named, gates, 0.0), axis=1)
        hits = hit.astype(jnp.int32).reshape(device_count, here)
        rank = (jnp.cumsum(hits, axis=1) - hits).reshape(-1)
        cell = places // here * capacity + rank
        cell = jnp.where(hit & (rank < capacity), cell, -1)
        placing = jnp.arange(slot_total, dtype=jnp.int32)[:, None] == cell[None, :]
        placing = placing.astype(BF16)
        hidden = dot(hidden_routed[e], placing, 0, 0)
        back = dot(down_routed[e], x, 1, 1) * weight[None, :]
        sums.append(jnp.sum(hidden * back, axis=0))
        gated = placing * gate.astype(BF16)[None, :]
        d_hidden.append(dot(gated, back.astype(BF16), 1, 1).astype(BF16))
        scaled = (hidden * (gate * weight)[None, :]).astype(BF16)
        d_down.append(dot(scaled, x, 1, 0).astype(BF16))
    slot_grad = jnp.stack(sums).reshape(experts, device_count, here)
    where = jnp.stack([node, lax.axis_index("local")]).astype(jnp.int32)
    d_gate = gates_call((node_count, local_count), exchanged(jnp.swapaxes(slot_grad, 0, 1)), expert_ids.T).T
    near_total = local_count * here
    near = lax.dynamic_slice_in_dim(x, node * near_total, near_total, 0)
    near_weight = lax.dynamic_slice_in_dim(weight, node * near_total, near_total, 0)
    shared_back = dot(near, down_shared, 1, 1)
    d_hidden_shared = (shared_back * near_weight[:, None]).astype(BF16)
    columns = features // node_count
    mine = lax.dynamic_slice_in_dim(x, node * columns, columns, 1)
    shared = lax.all_gather(hidden_shared, "node", axis=0, tiled=True)
    shared = (shared.astype(F32) * weight[:, None]).astype(BF16)
    d_down_shared = dot(shared, mine, 0, 0).astype(BF16)
    return (jnp.stack(d_hidden), jnp.stack(d_down), d_gate, d_hidden_shared, d_down_shared)


def body(
    out_grad,
    lengths,
    gate_weights,
    expert_ids,
    hidden_routed,
    down_routed,
    hidden_shared,
    down_shared,
):
    counts = lax.axis_size("node"), lax.axis_size("local")
    device_count = counts[0] * counts[1]
    here, features = out_grad.shape
    choices = expert_ids.shape[1]
    slot_total = hidden_routed.shape[1]
    capacity = slot_total // device_count
    where = jnp.stack([lax.axis_index("node"), lax.axis_index("local")]).astype(jnp.int32)
    up, down = ring_shift(*counts, 1), ring_shift(*counts, -1)

    def send(a, pairs):
        return lax.ppermute(a, AXES, pairs)

    def swapped(a):
        return lax.ppermute(a, "node", [(n, n ^ 1) for n in range(counts[0])])

    together = lax.optimization_barrier
    packed, where = together((pack_call(out_grad, gate_weights.T, expert_ids.T), where))
    forth, back, other = [packed], [packed], [swapped(packed)]
    weights, shared = weights_call(counts, lengths, where, hidden_shared)
    for step in range(3):
        forth.append(send(forth[-1], up))
        back.append(send(back[-1], down))
        other += [swapped(forth[-1]), swapped(back[-1])]
        if step == 0:
            back[-1], weights, shared = together((back[-1], weights, shared))
    own = [packed, forth[1], back[1], forth[2], back[2], forth[3], back[3]]
    early = [block for pair in zip(own[:4], other[:4]) for block in pair]
    first = half_call(
        counts, capacity, choices, 0, where, weights, early, down_routed, hidden_routed, None, None
    )
    rows, *first = first
    forth[3], back[3], first[3] = together((forth[3], back[3], first[3]))
    own[-2:] = forth[3], back[3]
    split = features // 2 // 128 * 128
    left, right = send(forth[3][:, :split], up), send(back[3][:, split:], down)
    across = lax.ppermute(shared, "node", [(n, n ^ 2) for n in range(counts[0])])
    shared = [shared, swapped(shared), across]
    d_hidden_shared = shared_back_call(counts, where, weights, own, down_shared)
    left, right, shared, d_hidden_shared = together((left, right, shared, d_hidden_shared))
    own.append(jnp.concatenate([left, right], axis=1))
    other.append(swapped(own[-1]))
    shared.append(swapped(shared[2]))
    late = [block for pair in zip(own[4:], other[4:]) for block in pair]
    second = half_call(
        counts, capacity, choices, len(early), where, weights, late, down_routed, hidden_routed, rows, first[3]
    )
    rows, *second = second
    d_gate = gates_call(counts, exchanged(second[3]), expert_ids.T).T
    d_down, d_hidden_routed, d_down_shared = last_call(
        counts, slot_total, where, rows, (None, *first[:3]), (None, *second[:3]), shared
    )
    return (d_hidden_routed, d_down, d_gate, d_hidden_shared, d_down_shared)


def solution(mesh):
    placed = (
        P(("groups", "node", "local"), None),
        P("groups"),
        P(("groups", "node", "local"), None),
        P(("groups", "node", "local"), None),
        P("node", "groups", "local"),
        P("node", "local", None),
        P(("groups", "node"), "local"),
        P("local", None),
    )
    small = mesh.shape["node"] == 4 and mesh.shape["local"] == 4
    return jax.shard_map(
        body if small else wide_body,
        mesh=mesh,
        in_specs=placed,
        out_specs=(
            P("node", "groups", "local"),
            P(("groups", "node"), "local", None),
            P(("groups", "node", "local"), None),
            P(("groups", "node"), "local"),
            P(("groups", "local"), "node"),
        ),
        check_vma=False,
    )
```

```python
import jax
import jax.numpy as jnp
from jax import lax
from jax.experimental import pallas as pl
from jax.experimental.pallas import tpu as pltpu
from jax.sharding import PartitionSpec as P

MEAN_LENGTH = 32.0
AXES = ("node", "local")
F32 = jnp.float32
BF16 = jnp.bfloat16


def dot(a, b, ca, cb):
    return lax.dot_general(a, b, (((ca,), (cb,)), ((), ())), preferred_element_type=F32)


def ring_places(node_count, local_count):
    chips = []
    for y in range(node_count // 2):
        row = range(local_count) if y % 2 == 0 else range(local_count - 1, -1, -1)
        chips += [(y, z) for z in row]
    return chips


def ring_shift(node_count, local_count, step):
    chips = ring_places(node_count, local_count)
    pairs = []
    for r, chip in enumerate(chips):
        to = chips[(r + step) % len(chips)]
        for core in (0, 1):
            pairs.append(
                ((chip[0] * 2 + core) * local_count + chip[1], (to[0] * 2 + core) * local_count + to[1])
            )
    return pairs


def block_numbers(node, local, node_count, local_count):
    total = node_count // 2 * local_count
    y, core = node // 2, node % 2
    mine = y * local_count + jnp.where(y % 2 == 0, local, local_count - 1 - local)
    offsets = [0]
    for step in range(1, (total - 1) // 2 + 1):
        offsets += [-step, step]
    offsets.append(total // 2)
    numbers = []
    for offset in offsets:
        at = (mine + offset + total) % total
        at_y, at_z = at // local_count, at % local_count
        at_z = jnp.where(at_y % 2 == 0, at_z, local_count - 1 - at_z)
        for at_core in (core, 1 - core):
            numbers.append((at_y * 2 + at_core) * local_count + at_z)
    return numbers


def lengths_at(lens_ref, tokens):
    found = jnp.zeros(tokens.shape, jnp.int32)
    end = 0
    for r in range(lens_ref.shape[0]):
        found = jnp.where(tokens >= end, lens_ref[r], found)
        end = end + lens_ref[r]
    return found.astype(F32)


VMEM = pl.BlockSpec(memory_space=pltpu.VMEM)
SMEM = pl.BlockSpec(memory_space=pltpu.SMEM)
ANY = pl.BlockSpec(memory_space=pl.ANY)
MIB = 2**20
WEIGHTS_FLOPS = 20 * 10**9
HALF_FLOPS = 6 * 10**9
SHARED_FLOPS = 3 * 10**9
PACK_MIB = 57
LAST_MIB = 40
ROWS_BYTES = 66 * MIB
LITTLE = pl.CostEstimate(flops=10**6, bytes_accessed=10**4, transcendentals=0)


def numbers_at(numbers, tokens, here):
    token = lax.broadcasted_iota(jnp.int32, (1, tokens), 1)
    found = jnp.zeros((1, tokens), jnp.int32)
    for b, number in enumerate(numbers):
        found = jnp.where(token >= b * here, number, found)
    return found


def pack_call(out_grad, gates, ids):
    here, features = out_grad.shape
    choices = gates.shape[0]

    def kernel(rows_ref, gates_ref, ids_ref, out_ref, gates_scr, ids_scr, sems):
        pairs = ((gates_ref, gates_scr), (ids_ref, ids_scr), (rows_ref, out_ref.at[:, :features]))
        copies = [pltpu.make_async_copy(a, b, sems.at[n]) for n, (a, b) in enumerate(pairs)]
        for copy in copies:
            copy.start()
        for copy in copies[:2]:
            copy.wait()
        pad = jnp.zeros((128 - 2 * choices, here), F32)
        tags = jnp.concatenate([gates_scr[...].astype(F32), ids_scr[...].astype(F32), pad], axis=0)
        out_ref[:, features:] = tags.T.astype(BF16)
        copies[2].wait()

    return pl.pallas_call(
        kernel,
        out_shape=jax.ShapeDtypeStruct((here, features + 128), BF16),
        in_specs=[ANY] * 3,
        out_specs=VMEM,
        scratch_shapes=[
            pltpu.VMEM(gates.shape, gates.dtype),
            pltpu.VMEM(ids.shape, ids.dtype),
            pltpu.SemaphoreType.DMA((3,)),
        ],
        compiler_params=pltpu.CompilerParams(vmem_limit_bytes=PACK_MIB * MIB),
        cost_estimate=LITTLE,
        name="pack",
    )(out_grad, gates, ids)


def weights_call(counts, lengths, where, shared, hidden):
    experts, slot_total, units = hidden.shape
    node_tokens, _ = shared.shape
    here = node_tokens // counts[1]
    tokens = counts[0] * node_tokens

    def kernel(lens_ref, where_ref, shared_ref, hidden_ref, weight_ref, out_ref, turned_ref):
        for e in range(experts):
            turned_ref[e] = hidden_ref[e].astype(F32).T.astype(BF16)
        node, local = where_ref[0], where_ref[1]
        number = numbers_at(block_numbers(node, local, *counts), tokens, here)
        token = lax.broadcasted_iota(jnp.int32, (1, tokens), 1)
        row = lax.broadcasted_iota(jnp.int32, (8, tokens), 0)
        weight = MEAN_LENGTH / lengths_at(lens_ref, number * here + token % here)
        near = MEAN_LENGTH / lengths_at(lens_ref, node * node_tokens + token % node_tokens)
        weight_ref[...] = jnp.where(row == 0, weight, near)
        spread = lax.broadcasted_iota(jnp.int32, (node_tokens, 128), 0)
        column = MEAN_LENGTH / lengths_at(lens_ref, node * node_tokens + spread)[:, :1]
        out_ref[...] = (shared_ref[...].astype(F32) * column).astype(BF16)

    return pl.pallas_call(
        kernel,
        out_shape=(
            jax.ShapeDtypeStruct((8, tokens), F32),
            jax.ShapeDtypeStruct(shared.shape, BF16),
            jax.ShapeDtypeStruct((experts, units, slot_total), BF16),
        ),
        in_specs=[SMEM, SMEM, VMEM, VMEM],
        out_specs=[VMEM] * 3,
        compiler_params=pltpu.CompilerParams(vmem_limit_bytes=8 * MIB),
        cost_estimate=pl.CostEstimate(flops=WEIGHTS_FLOPS, bytes_accessed=10**6, transcendentals=0),
        name="weights",
    )(lengths, where, shared, hidden)


def place(node, numbers, capacity, blocks, weight, hidden_ref, features, choices):
    here = blocks[0].shape[0]
    tokens = here * len(blocks)
    experts, _, slot_total = hidden_ref.shape
    tags = jnp.concatenate([block[:, features:] for block in blocks], axis=0).astype(F32).T
    gates, ids = tags[:choices], tags[choices : 2 * choices]
    number = numbers_at(numbers, tokens, here).astype(F32)
    token = lax.broadcasted_iota(jnp.int32, (1, tokens), 1)
    first = token - token % here
    down = lax.broadcasted_iota(jnp.int32, (tokens, 1), 0)
    earlier = ((down < token) & (down >= first)).astype(F32).astype(BF16)
    named = [ids == (node * experts + e).astype(F32) for e in range(experts)]
    hits = [jnp.sum(n.astype(F32), axis=0, keepdims=True) for n in named]
    gate = [jnp.sum(jnp.where(n, gates, 0.0), axis=0, keepdims=True) for n in named]
    row = lax.broadcasted_iota(jnp.int32, (8, tokens), 0)
    stacked = jnp.zeros((8, tokens), F32)
    for e in range(experts):
        stacked = jnp.where(row == e, hits[e], stacked)
    ranks = dot(stacked.astype(BF16), earlier, 1, 0)
    slot = lax.broadcasted_iota(jnp.int32, (slot_total, 1), 0).astype(F32)
    info = jnp.zeros((8, tokens), F32)
    placed, scaled = [], []
    for e in range(experts):
        rank = ranks[e : e + 1]
        live = (hits[e] > 0.5) & (rank < capacity - 0.5)
        cell = jnp.where(live, number * capacity + rank, -1.0)
        info = jnp.where(row == e, cell, info)
        info = jnp.where(row == experts + e, gate[e], info)
        placing = (slot == cell).astype(F32).astype(BF16)
        hidden = dot(hidden_ref[e], placing, 1, 0)
        placed.append(hidden.astype(BF16))
        scaled.append((hidden * (gate[e] * weight)).astype(BF16))
    return info, placed, scaled


def half_call(counts, capacity, choices, start, where, weights, blocks, down, hidden, rows, sums):
    experts, units, features = down.shape
    count, here = len(blocks), blocks[0].shape[0]
    tokens = here * count
    device_count = counts[0] * counts[1]
    first = start * here
    step = 256 if units % 256 == 0 else units
    more = [] if rows is None else [rows, sums]

    def kernel(where_ref, *refs):
        blocks, (weights_ref, down_ref, hidden_ref), refs = refs[:count], refs[count : count + 3], refs[count + 3 :]
        before, refs = refs[: len(more)], refs[len(more) :]
        rows_ref, grad_ref, scaled_ref, info_ref, sums_ref, x_scr, grad_scr, scaled_scr, placed_scr, sems = refs
        copies = []

        def write(scr, ref):
            copies.append(pltpu.make_async_copy(scr, ref, sems.at[len(copies)]))
            copies[-1].start()

        node, local = where_ref[0], where_ref[1]
        numbers = block_numbers(node, local, *counts)[start : start + count]
        for b, block in enumerate(blocks):
            x_scr[b * here : (b + 1) * here, :] = block[:, :features]
        write(x_scr, rows_ref.at[pl.ds(first, tokens)])
        weight = weights_ref[:1, first : first + tokens]
        info, placed, scaled = place(node, numbers, capacity, blocks, weight, hidden_ref, features, choices)
        info_ref[...] = info
        for e in range(experts):
            scaled_scr[e] = scaled[e]
            placed_scr[e] = placed[e]
        write(scaled_scr, scaled_ref)
        row = lax.broadcasted_iota(jnp.int32, (8, tokens), 0)
        total = jnp.zeros((8, tokens), F32)
        for e in range(experts):
            for i in range(0, units, step):
                at = slice(i, i + step)
                back = dot(down_ref[e, at, :], x_scr[...], 1, 1) * weight
                grad_scr[e, at, :] = back.astype(BF16)
                found = jnp.sum(back * placed_scr[e, at, :].astype(F32), axis=0, keepdims=True)
                total = total + jnp.where(row == e, found, 0.0)
            write(grad_scr.at[e], grad_ref.at[e])
        if more:
            sums_ref[...] = before[1][...]
        else:
            sums_ref[...] = jnp.zeros(sums_ref.shape, F32)
        for b, number in enumerate(numbers):
            sums_ref[number] = total[:experts, b * here : (b + 1) * here]
        for copy in copies:
            copy.wait()

    return pl.pallas_call(
        kernel,
        out_shape=(
            jax.ShapeDtypeStruct((-(-ROWS_BYTES // (2 * features)), features), BF16),
            jax.ShapeDtypeStruct((experts, units, tokens), BF16),
            jax.ShapeDtypeStruct((experts, units, tokens), BF16),
            jax.ShapeDtypeStruct((8, tokens), F32),
            jax.ShapeDtypeStruct((device_count, experts, here), F32),
        ),
        in_specs=[SMEM] + [VMEM] * (count + 3) + [ANY, VMEM][: len(more)],
        out_specs=[ANY, ANY, ANY, VMEM, VMEM],
        input_output_aliases={count + 4: 0} if more else {},
        scratch_shapes=[
            pltpu.VMEM((tokens, features), BF16),
            pltpu.VMEM((experts, units, tokens), BF16),
            pltpu.VMEM((experts, units, tokens), BF16),
            pltpu.VMEM((experts, units, tokens), BF16),
            pltpu.SemaphoreType.DMA((2 + experts,)),
        ],
        compiler_params=pltpu.CompilerParams(vmem_limit_bytes=12 * MIB),
        cost_estimate=pl.CostEstimate(flops=HALF_FLOPS, bytes_accessed=10**6, transcendentals=0),
        name="half_second" if more else "half_first",
    )(where, *blocks, weights, down, hidden, *more)


def last_call(counts, slot_total, where, rows, first, second, shared):
    experts, units, tokens = first[1].shape
    features = rows.shape[1]
    node_tokens, shared_units = shared[0].shape
    width = features // counts[0]
    here = node_tokens // counts[1]
    step = 256 if units % 256 == 0 else units
    parts = units // step

    def kernel(where_ref, rows_ref, *refs):
        given, (info_a, info_b), shared, refs = refs[:4], refs[4:6], refs[6:10], refs[10:]
        down_ref, hidden_ref, shared_ref = refs[:3]
        x_scr, grad_scr, scaled_scr, all_scr, ordered_scr, down_scr, hidden_scr, shared_scr, sems, out_sems = refs[3:]
        loads, copies = [], []

        def load(ref, scr):
            loads.append(pltpu.make_async_copy(ref, scr, sems.at[len(loads)]))
            loads[-1].start()

        def write(scr, ref):
            copies.append(pltpu.make_async_copy(scr, ref, out_sems.at[len(copies)]))
            copies[-1].start()

        for ref, scr in zip(given, (grad_scr, grad_scr, scaled_scr, scaled_scr)):
            load(ref, scr.at[:, :, pl.ds(len(loads) % 2 * tokens, tokens)])
        for n in range(2):
            at = pl.ds(n * (features // 2), features // 2)
            load(rows_ref.at[pl.ds(0, 2 * tokens), at], x_scr.at[:, at])
        node, local = where_ref[0], where_ref[1]
        for n, part in enumerate(shared):
            at = pl.multiple_of((node ^ n) * node_tokens, node_tokens)
            all_scr[pl.ds(at, node_tokens), :] = part[...]
        for b, number in enumerate(block_numbers(node, local, *counts)):
            of = pl.ds(pl.multiple_of(number * here, here), here)
            ordered_scr[b * here : (b + 1) * here, :] = all_scr[of, :]
        slot = lax.broadcasted_iota(jnp.int32, (slot_total, 1), 0).astype(F32)

        def by_slot(e):
            gated = []
            for info in (info_a, info_b):
                gate = info[experts + e : experts + e + 1, :]
                gated.append(jnp.where(slot == info[e : e + 1, :], gate, 0.0).astype(BF16))
            hidden_scr[e] = dot(jnp.concatenate(gated, axis=1), grad_scr[e], 1, 1).astype(BF16)
            write(hidden_scr.at[e], hidden_ref.at[e])

        for copy in loads[:2]:
            copy.wait()
        for e in range(experts):
            by_slot(e)
        for copy in loads[2:4]:
            copy.wait()
        for e in range(experts):
            for n in range(parts):
                at = slice(n * step, (n + 1) * step)
                place = down_scr.at[e * parts + n]
                for half in range(2):
                    if e == n == 0:
                        loads[4 + half].wait()
                    columns = slice(half * (features // 2), (half + 1) * (features // 2))
                    place[:, columns] = dot(scaled_scr[e, at, :], x_scr[:, columns], 1, 0).astype(BF16)
                write(place, down_ref.at[e, pl.ds(n * step, step)])
        columns = pl.ds(pl.multiple_of(node * width, width), width)
        shared_scr[...] = dot(ordered_scr[...], x_scr[:, columns], 0, 0).astype(BF16)
        write(shared_scr, shared_ref)
        for copy in copies:
            copy.wait()

    return pl.pallas_call(
        kernel,
        out_shape=(
            jax.ShapeDtypeStruct((experts, units, features), BF16),
            jax.ShapeDtypeStruct((experts, slot_total, units), BF16),
            jax.ShapeDtypeStruct((shared_units, width), BF16),
        ),
        in_specs=[SMEM] + [ANY] * 5 + [VMEM] * 6,
        out_specs=[ANY] * 3,
        scratch_shapes=[
            pltpu.VMEM((2 * tokens, features), BF16),
            pltpu.VMEM((experts, units, 2 * tokens), BF16),
            pltpu.VMEM((experts, units, 2 * tokens), BF16),
            pltpu.VMEM((4 * node_tokens, shared_units), BF16),
            pltpu.VMEM((4 * node_tokens, shared_units), BF16),
            pltpu.VMEM((experts * parts, step, features), BF16),
            pltpu.VMEM((experts, slot_total, units), BF16),
            pltpu.VMEM((shared_units, width), BF16),
            pltpu.SemaphoreType.DMA((6,)),
            pltpu.SemaphoreType.DMA((experts * parts + experts + 1,)),
        ],
        compiler_params=pltpu.CompilerParams(vmem_limit_bytes=LAST_MIB * MIB),
        cost_estimate=pl.CostEstimate(flops=8 * 10**9, bytes_accessed=10**7, transcendentals=0),
        name="last",
    )(where, rows, first[1], second[1], first[2], second[2], first[3], second[3], *shared)


def shared_back_call(counts, where, weights, blocks, down):
    units, features = down.shape
    here = blocks[0].shape[0]
    tokens = here * counts[1]

    def kernel(where_ref, *refs):
        blocks, (weights_ref, down_ref, out_ref, near_scr) = refs[:-4], refs[-4:]
        node, local = where_ref[0], where_ref[1]
        for block, number in zip(blocks, block_numbers(node, local, *counts)[::2]):

            @pl.when(number // counts[1] == node)
            def _(block=block, number=number):
                to = pl.ds(pl.multiple_of(number % counts[1] * here, here), here)
                near_scr[to, :] = block[:, :features]

        back = dot(down_ref[...], near_scr[...], 1, 1) * weights_ref[1:2, :tokens]
        out_ref[...] = back.T.astype(BF16)

    return pl.pallas_call(
        kernel,
        out_shape=jax.ShapeDtypeStruct((tokens, units), BF16),
        in_specs=[SMEM] + [VMEM] * (len(blocks) + 2),
        out_specs=VMEM,
        scratch_shapes=[pltpu.VMEM((tokens, features), BF16)],
        compiler_params=pltpu.CompilerParams(vmem_limit_bytes=12 * MIB),
        cost_estimate=pl.CostEstimate(flops=SHARED_FLOPS, bytes_accessed=10**6, transcendentals=0),
        name="shared_back",
    )(where, *blocks, weights, down)


def gates_call(counts, parts, ids):
    experts = parts.shape[1]

    def kernel(ids_ref, parts_ref, out_ref):
        d_gate = jnp.zeros(out_ref.shape, F32)
        for node in range(counts[0]):
            total = parts_ref[node * counts[1]]
            for local in range(1, counts[1]):
                total = total + parts_ref[node * counts[1] + local]
            for e in range(experts):
                d_gate = d_gate + jnp.where(ids_ref[...] == node * experts + e, total[e : e + 1], 0.0)
        out_ref[...] = d_gate

    return pl.pallas_call(
        kernel,
        out_shape=jax.ShapeDtypeStruct(ids.shape, F32),
        in_specs=[VMEM] * 2,
        out_specs=VMEM,
        compiler_params=pltpu.CompilerParams(vmem_limit_bytes=4 * MIB),
        cost_estimate=LITTLE,
        name="gates",
    )(ids, parts)


def exchanged(a):
    return lax.all_to_all(a, AXES, split_axis=0, concat_axis=0, tiled=True)


def wide_body(
    out_grad,
    lengths,
    gate_weights,
    expert_ids,
    hidden_routed,
    down_routed,
    hidden_shared,
    down_shared,
):
    node_count = lax.axis_size("node")
    local_count = lax.axis_size("local")
    device_count = node_count * local_count
    here, features = out_grad.shape
    choices = expert_ids.shape[1]
    experts, slot_total, units = hidden_routed.shape
    capacity = slot_total // device_count
    node = lax.axis_index("node")
    pad = jnp.zeros((here, 128 - 2 * choices), BF16)
    packed = jnp.concatenate([out_grad, gate_weights, expert_ids.astype(BF16), pad], axis=1)
    rows = lax.all_gather(packed, AXES, axis=0, tiled=True)
    token_total = device_count * here
    ends = jnp.cumsum(lengths)
    places = jnp.arange(token_total, dtype=jnp.int32)
    inside = (places[:, None] >= (ends - lengths)[None, :]) & (places[:, None] < ends[None, :])
    weight = MEAN_LENGTH / jnp.sum(jnp.where(inside, lengths[None, :], 0), axis=1).astype(F32)
    x = rows[:, :features]
    gates = rows[:, features : features + choices].astype(F32)
    ids = rows[:, features + choices : features + 2 * choices].astype(jnp.int32)
    d_hidden, d_down, sums = [], [], []
    for e in range(experts):
        named = ids == node * experts + e
        hit = jnp.any(named, axis=1)
        gate = jnp.sum(jnp.where(named, gates, 0.0), axis=1)
        hits = hit.astype(jnp.int32).reshape(device_count, here)
        rank = (jnp.cumsum(hits, axis=1) - hits).reshape(-1)
        cell = places // here * capacity + rank
        cell = jnp.where(hit & (rank < capacity), cell, -1)
        placing = jnp.arange(slot_total, dtype=jnp.int32)[:, None] == cell[None, :]
        placing = placing.astype(BF16)
        hidden = dot(hidden_routed[e], placing, 0, 0)
        back = dot(down_routed[e], x, 1, 1) * weight[None, :]
        sums.append(jnp.sum(hidden * back, axis=0))
        gated = placing * gate.astype(BF16)[None, :]
        d_hidden.append(dot(gated, back.astype(BF16), 1, 1).astype(BF16))
        scaled = (hidden * (gate * weight)[None, :]).astype(BF16)
        d_down.append(dot(scaled, x, 1, 0).astype(BF16))
    slot_grad = jnp.stack(sums).reshape(experts, device_count, here)
    where = jnp.stack([node, lax.axis_index("local")]).astype(jnp.int32)
    d_gate = gates_call((node_count, local_count), exchanged(jnp.swapaxes(slot_grad, 0, 1)), expert_ids.T).T
    near_total = local_count * here
    near = lax.dynamic_slice_in_dim(x, node * near_total, near_total, 0)
    near_weight = lax.dynamic_slice_in_dim(weight, node * near_total, near_total, 0)
    shared_back = dot(near, down_shared, 1, 1)
    d_hidden_shared = (shared_back * near_weight[:, None]).astype(BF16)
    columns = features // node_count
    mine = lax.dynamic_slice_in_dim(x, node * columns, columns, 1)
    shared = lax.all_gather(hidden_shared, "node", axis=0, tiled=True)
    shared = (shared.astype(F32) * weight[:, None]).astype(BF16)
    d_down_shared = dot(shared, mine, 0, 0).astype(BF16)
    return (jnp.stack(d_hidden), jnp.stack(d_down), d_gate, d_hidden_shared, d_down_shared)


def body(
    out_grad,
    lengths,
    gate_weights,
    expert_ids,
    hidden_routed,
    down_routed,
    hidden_shared,
    down_shared,
):
    counts = lax.axis_size("node"), lax.axis_size("local")
    device_count = counts[0] * counts[1]
    here, features = out_grad.shape
    choices = expert_ids.shape[1]
    slot_total = hidden_routed.shape[1]
    capacity = slot_total // device_count
    where = jnp.stack([lax.axis_index("node"), lax.axis_index("local")]).astype(jnp.int32)
    up, down = ring_shift(*counts, 1), ring_shift(*counts, -1)

    def send(a, pairs):
        return lax.ppermute(a, AXES, pairs)

    def swapped(a):
        return lax.ppermute(a, "node", [(n, n ^ 1) for n in range(counts[0])])

    together = lax.optimization_barrier
    packed, where = together((pack_call(out_grad, gate_weights.T, expert_ids.T), where))
    forth, back, other = [packed], [packed], [swapped(packed)]
    weights, shared, turned = weights_call(counts, lengths, where, hidden_shared, hidden_routed)
    for step in range(3):
        forth.append(send(forth[-1], up))
        back.append(send(back[-1], down))
        other += [swapped(forth[-1]), swapped(back[-1])]
        if step == 0:
            forth[-1], weights, shared, turned = together((forth[-1], weights, shared, turned))
            shared = [shared, swapped(shared)]
        if step == 1:
            forth[-1], shared = together((forth[-1], shared))
    own = [packed, forth[1], back[1], forth[2], back[2], forth[3], back[3]]
    early = [block for pair in zip(own[:4], other[:4]) for block in pair]
    first = half_call(
        counts, capacity, choices, 0, where, weights, early, down_routed, turned, None, None
    )
    rows, *first = first
    forth[3], back[3], first[3] = together((forth[3], back[3], first[3]))
    own[-2:] = forth[3], back[3]
    split = features // 2 // 128 * 128
    left, right = send(forth[3][:, :split], up), send(back[3][:, split:], down)
    d_hidden_shared = shared_back_call(counts, where, weights, own, down_shared)
    left, right, shared, d_hidden_shared = together((left, right, shared, d_hidden_shared))
    own.append(jnp.concatenate([left, right], axis=1))
    other.append(swapped(own[-1]))
    shared.append(lax.ppermute(shared[0], "node", [(n, n ^ 2) for n in range(counts[0])]))
    late = [block for pair in zip(own[4:], other[4:]) for block in pair]
    second = half_call(
        counts, capacity, choices, len(early), where, weights, late, down_routed, turned, rows, first[3]
    )
    rows, *second = second
    second[3], shared[2] = together((second[3], shared[2]))
    shared.append(swapped(shared[2]))
    parts = exchanged(second[3])
    d_down, d_hidden_routed, d_down_shared = last_call(
        counts, slot_total, where, rows, (None, *first[:3]), (None, *second[:3]), shared
    )
    parts, d_down_shared = together((parts, d_down_shared))
    d_gate = gates_call(counts, parts, expert_ids.T).T
    return (d_hidden_routed, d_down, d_gate, d_hidden_shared, d_down_shared)


def solution(mesh):
    placed = (
        P(("groups", "node", "local"), None),
        P("groups"),
        P(("groups", "node", "local"), None),
        P(("groups", "node", "local"), None),
        P("node", "groups", "local"),
        P("node", "local", None),
        P(("groups", "node"), "local"),
        P("local", None),
    )
    small = mesh.shape["node"] == 4 and mesh.shape["local"] == 4
    return jax.shard_map(
        body if small else wide_body,
        mesh=mesh,
        in_specs=placed,
        out_specs=(
            P("node", "groups", "local"),
            P(("groups", "node"), "local", None),
            P(("groups", "node", "local"), None),
            P(("groups", "node"), "local"),
            P(("groups", "local"), "node"),
        ),
        check_vma=False,
    )
```

```python
import jax
import jax.numpy as jnp
from jax import lax
from jax.experimental import pallas as pl
from jax.experimental.pallas import tpu as pltpu
from jax.sharding import PartitionSpec as P

MEAN_LENGTH = 32.0
AXES = ("node", "local")
F32 = jnp.float32
BF16 = jnp.bfloat16


def dot(a, b, ca, cb):
    return lax.dot_general(a, b, (((ca,), (cb,)), ((), ())), preferred_element_type=F32)


def ring_places(node_count, local_count):
    chips = []
    for y in range(node_count // 2):
        row = range(local_count) if y % 2 == 0 else range(local_count - 1, -1, -1)
        chips += [(y, z) for z in row]
    return chips


def ring_shift(node_count, local_count, step):
    chips = ring_places(node_count, local_count)
    pairs = []
    for r, chip in enumerate(chips):
        to = chips[(r + step) % len(chips)]
        for core in (0, 1):
            pairs.append(
                ((chip[0] * 2 + core) * local_count + chip[1], (to[0] * 2 + core) * local_count + to[1])
            )
    return pairs


def block_numbers(node, local, node_count, local_count):
    total = node_count // 2 * local_count
    y, core = node // 2, node % 2
    mine = y * local_count + jnp.where(y % 2 == 0, local, local_count - 1 - local)
    offsets = [0]
    for step in range(1, (total - 1) // 2 + 1):
        offsets += [-step, step]
    offsets.append(total // 2)
    numbers = []
    for offset in offsets:
        at = (mine + offset + total) % total
        at_y, at_z = at // local_count, at % local_count
        at_z = jnp.where(at_y % 2 == 0, at_z, local_count - 1 - at_z)
        for at_core in (core, 1 - core):
            numbers.append((at_y * 2 + at_core) * local_count + at_z)
    return numbers


def lengths_at(lens_ref, tokens):
    found = jnp.zeros(tokens.shape, jnp.int32)
    end = 0
    for r in range(lens_ref.shape[0]):
        found = jnp.where(tokens >= end, lens_ref[r], found)
        end = end + lens_ref[r]
    return found.astype(F32)


VMEM = pl.BlockSpec(memory_space=pltpu.VMEM)
SMEM = pl.BlockSpec(memory_space=pltpu.SMEM)
ANY = pl.BlockSpec(memory_space=pl.ANY)
MIB = 2**20
WEIGHTS_FLOPS = 20 * 10**9
HALF_FLOPS = 6 * 10**9
SHARED_FLOPS = 3 * 10**9
PACK_MIB = 57
LAST_MIB = 40
ROWS_BYTES = 66 * MIB
LITTLE = pl.CostEstimate(flops=10**6, bytes_accessed=10**4, transcendentals=0)


def numbers_at(numbers, tokens, here):
    token = lax.broadcasted_iota(jnp.int32, (1, tokens), 1)
    found = jnp.zeros((1, tokens), jnp.int32)
    for b, number in enumerate(numbers):
        found = jnp.where(token >= b * here, number, found)
    return found


def pack_call(out_grad, gates, ids):
    here, features = out_grad.shape
    choices = gates.shape[0]

    def kernel(rows_ref, gates_ref, ids_ref, out_ref, gates_scr, ids_scr, sems):
        pairs = ((gates_ref, gates_scr), (ids_ref, ids_scr), (rows_ref, out_ref.at[:, :features]))
        copies = [pltpu.make_async_copy(a, b, sems.at[n]) for n, (a, b) in enumerate(pairs)]
        for copy in copies:
            copy.start()
        for copy in copies[:2]:
            copy.wait()
        pad = jnp.zeros((128 - 2 * choices, here), F32)
        tags = jnp.concatenate([gates_scr[...].astype(F32), ids_scr[...].astype(F32), pad], axis=0)
        out_ref[:, features:] = tags.T.astype(BF16)
        copies[2].wait()

    return pl.pallas_call(
        kernel,
        out_shape=jax.ShapeDtypeStruct((here, features + 128), BF16),
        in_specs=[ANY] * 3,
        out_specs=VMEM,
        scratch_shapes=[
            pltpu.VMEM(gates.shape, gates.dtype),
            pltpu.VMEM(ids.shape, ids.dtype),
            pltpu.SemaphoreType.DMA((3,)),
        ],
        compiler_params=pltpu.CompilerParams(vmem_limit_bytes=PACK_MIB * MIB),
        cost_estimate=LITTLE,
        name="pack",
    )(out_grad, gates, ids)


def weights_call(counts, lengths, where, shared, hidden):
    experts, slot_total, units = hidden.shape
    node_tokens, _ = shared.shape
    here = node_tokens // counts[1]
    tokens = counts[0] * node_tokens

    def kernel(lens_ref, where_ref, shared_ref, hidden_ref, weight_ref, out_ref, turned_ref):
        for e in range(experts):
            turned_ref[e] = hidden_ref[e].astype(F32).T.astype(BF16)
        node, local = where_ref[0], where_ref[1]
        number = numbers_at(block_numbers(node, local, *counts), tokens, here)
        token = lax.broadcasted_iota(jnp.int32, (1, tokens), 1)
        row = lax.broadcasted_iota(jnp.int32, (8, tokens), 0)
        weight = MEAN_LENGTH / lengths_at(lens_ref, number * here + token % here)
        near = MEAN_LENGTH / lengths_at(lens_ref, node * node_tokens + token % node_tokens)
        weight_ref[...] = jnp.where(row == 0, weight, near)
        spread = lax.broadcasted_iota(jnp.int32, (node_tokens, 128), 0)
        column = MEAN_LENGTH / lengths_at(lens_ref, node * node_tokens + spread)[:, :1]
        out_ref[...] = (shared_ref[...].astype(F32) * column).astype(BF16)

    return pl.pallas_call(
        kernel,
        out_shape=(
            jax.ShapeDtypeStruct((8, tokens), F32),
            jax.ShapeDtypeStruct(shared.shape, BF16),
            jax.ShapeDtypeStruct((experts, units, slot_total), BF16),
        ),
        in_specs=[SMEM, SMEM, VMEM, VMEM],
        out_specs=[VMEM] * 3,
        compiler_params=pltpu.CompilerParams(vmem_limit_bytes=8 * MIB),
        cost_estimate=pl.CostEstimate(flops=WEIGHTS_FLOPS, bytes_accessed=10**6, transcendentals=0),
        name="weights",
    )(lengths, where, shared, hidden)


def place(node, numbers, capacity, blocks, weight, hidden_ref, features, choices):
    here = blocks[0].shape[0]
    tokens = here * len(blocks)
    experts, _, slot_total = hidden_ref.shape
    tags = jnp.concatenate([block[:, features:] for block in blocks], axis=0).astype(F32).T
    gates, ids = tags[:choices], tags[choices : 2 * choices]
    number = numbers_at(numbers, tokens, here).astype(F32)
    token = lax.broadcasted_iota(jnp.int32, (1, tokens), 1)
    first = token - token % here
    down = lax.broadcasted_iota(jnp.int32, (tokens, 1), 0)
    earlier = ((down < token) & (down >= first)).astype(F32).astype(BF16)
    named = [ids == (node * experts + e).astype(F32) for e in range(experts)]
    hits = [jnp.sum(n.astype(F32), axis=0, keepdims=True) for n in named]
    gate = [jnp.sum(jnp.where(n, gates, 0.0), axis=0, keepdims=True) for n in named]
    row = lax.broadcasted_iota(jnp.int32, (8, tokens), 0)
    stacked = jnp.zeros((8, tokens), F32)
    for e in range(experts):
        stacked = jnp.where(row == e, hits[e], stacked)
    ranks = dot(stacked.astype(BF16), earlier, 1, 0)
    slot = lax.broadcasted_iota(jnp.int32, (slot_total, 1), 0).astype(F32)
    info = jnp.zeros((8, tokens), F32)
    placed, scaled = [], []
    for e in range(experts):
        rank = ranks[e : e + 1]
        live = (hits[e] > 0.5) & (rank < capacity - 0.5)
        cell = jnp.where(live, number * capacity + rank, -1.0)
        info = jnp.where(row == e, cell, info)
        info = jnp.where(row == experts + e, gate[e], info)
        placing = (slot == cell).astype(F32).astype(BF16)
        hidden = dot(hidden_ref[e], placing, 1, 0)
        placed.append(hidden.astype(BF16))
        scaled.append((hidden * (gate[e] * weight)).astype(BF16))
    return info, placed, scaled


def half_call(counts, capacity, choices, start, where, weights, blocks, down, hidden, rows, sums):
    experts, units, features = down.shape
    count, here = len(blocks), blocks[0].shape[0]
    tokens = here * count
    device_count = counts[0] * counts[1]
    first = start * here
    step = 256 if units % 256 == 0 else units
    more = [] if rows is None else [rows, sums]

    def kernel(where_ref, *refs):
        blocks, (weights_ref, down_ref, hidden_ref), refs = refs[:count], refs[count : count + 3], refs[count + 3 :]
        before, refs = refs[: len(more)], refs[len(more) :]
        rows_ref, grad_ref, scaled_ref, info_ref, sums_ref, x_scr, grad_scr, scaled_scr, placed_scr, sems = refs
        copies = []

        def write(scr, ref):
            copies.append(pltpu.make_async_copy(scr, ref, sems.at[len(copies)]))
            copies[-1].start()

        node, local = where_ref[0], where_ref[1]
        numbers = block_numbers(node, local, *counts)[start : start + count]
        for b, block in enumerate(blocks):
            x_scr[b * here : (b + 1) * here, :] = block[:, :features]
        write(x_scr, rows_ref.at[pl.ds(first, tokens)])
        weight = weights_ref[:1, first : first + tokens]
        info, placed, scaled = place(node, numbers, capacity, blocks, weight, hidden_ref, features, choices)
        info_ref[...] = info
        for e in range(experts):
            scaled_scr[e] = scaled[e]
            placed_scr[e] = placed[e]
        write(scaled_scr, scaled_ref)
        row = lax.broadcasted_iota(jnp.int32, (8, tokens), 0)
        total = jnp.zeros((8, tokens), F32)
        for e in range(experts):
            for i in range(0, units, step):
                at = slice(i, i + step)
                back = dot(down_ref[e, at, :], x_scr[...], 1, 1) * weight
                grad_scr[e, at, :] = back.astype(BF16)
                found = jnp.sum(back * placed_scr[e, at, :].astype(F32), axis=0, keepdims=True)
                total = total + jnp.where(row == e, found, 0.0)
            write(grad_scr.at[e], grad_ref.at[e])
        if more:
            sums_ref[...] = before[1][...]
        else:
            sums_ref[...] = jnp.zeros(sums_ref.shape, F32)
        for b, number in enumerate(numbers):
            sums_ref[number] = total[:experts, b * here : (b + 1) * here]
        for copy in copies:
            copy.wait()

    return pl.pallas_call(
        kernel,
        out_shape=(
            jax.ShapeDtypeStruct((-(-ROWS_BYTES // (2 * features)), features), BF16),
            jax.ShapeDtypeStruct((experts, units, tokens), BF16),
            jax.ShapeDtypeStruct((experts, units, tokens), BF16),
            jax.ShapeDtypeStruct((8, tokens), F32),
            jax.ShapeDtypeStruct((device_count, experts, here), F32),
        ),
        in_specs=[SMEM] + [VMEM] * (count + 3) + [ANY, VMEM][: len(more)],
        out_specs=[ANY, ANY, ANY, VMEM, VMEM],
        input_output_aliases={count + 4: 0} if more else {},
        scratch_shapes=[
            pltpu.VMEM((tokens, features), BF16),
            pltpu.VMEM((experts, units, tokens), BF16),
            pltpu.VMEM((experts, units, tokens), BF16),
            pltpu.VMEM((experts, units, tokens), BF16),
            pltpu.SemaphoreType.DMA((2 + experts,)),
        ],
        compiler_params=pltpu.CompilerParams(vmem_limit_bytes=12 * MIB),
        cost_estimate=pl.CostEstimate(flops=HALF_FLOPS, bytes_accessed=10**6, transcendentals=0),
        name="half_second" if more else "half_first",
    )(where, *blocks, weights, down, hidden, *more)


def last_call(counts, slot_total, where, rows, first, second, shared):
    experts, units, tokens = first[1].shape
    features = rows.shape[1]
    node_tokens, shared_units = shared[0].shape
    width = features // counts[0]
    here = node_tokens // counts[1]
    step = 256 if units % 256 == 0 else units
    parts = units // step

    def kernel(where_ref, rows_ref, *refs):
        given, (info_a, info_b), shared, refs = refs[:4], refs[4:6], refs[6:10], refs[10:]
        down_ref, hidden_ref, shared_ref = refs[:3]
        x_scr, grad_scr, scaled_scr, all_scr, ordered_scr, down_scr, hidden_scr, shared_scr, sems, out_sems = refs[3:]
        loads, copies = [], []

        def load(ref, scr):
            loads.append(pltpu.make_async_copy(ref, scr, sems.at[len(loads)]))
            loads[-1].start()

        def write(scr, ref):
            copies.append(pltpu.make_async_copy(scr, ref, out_sems.at[len(copies)]))
            copies[-1].start()

        for ref, scr in zip(given, (grad_scr, grad_scr, scaled_scr, scaled_scr)):
            load(ref, scr.at[:, :, pl.ds(len(loads) % 2 * tokens, tokens)])
        for n in range(2):
            at = pl.ds(n * (features // 2), features // 2)
            load(rows_ref.at[pl.ds(0, 2 * tokens), at], x_scr.at[:, at])
        node, local = where_ref[0], where_ref[1]
        for n, part in enumerate(shared):
            at = pl.multiple_of((node ^ n) * node_tokens, node_tokens)
            all_scr[pl.ds(at, node_tokens), :] = part[...]
        for b, number in enumerate(block_numbers(node, local, *counts)):
            of = pl.ds(pl.multiple_of(number * here, here), here)
            ordered_scr[b * here : (b + 1) * here, :] = all_scr[of, :]
        slot = lax.broadcasted_iota(jnp.int32, (slot_total, 1), 0).astype(F32)

        def by_slot(e):
            gated = []
            for info in (info_a, info_b):
                gate = info[experts + e : experts + e + 1, :]
                gated.append(jnp.where(slot == info[e : e + 1, :], gate, 0.0).astype(BF16))
            hidden_scr[e] = dot(jnp.concatenate(gated, axis=1), grad_scr[e], 1, 1).astype(BF16)
            write(hidden_scr.at[e], hidden_ref.at[e])

        for copy in loads[:2]:
            copy.wait()
        for e in range(experts):
            by_slot(e)
        for copy in loads[2:4]:
            copy.wait()
        for e in range(experts):
            for n in range(parts):
                at = slice(n * step, (n + 1) * step)
                place = down_scr.at[e * parts + n]
                for half in range(2):
                    if e == n == 0:
                        loads[4 + half].wait()
                    columns = slice(half * (features // 2), (half + 1) * (features // 2))
                    place[:, columns] = dot(scaled_scr[e, at, :], x_scr[:, columns], 1, 0).astype(BF16)
                write(place, down_ref.at[e, pl.ds(n * step, step)])
        columns = pl.ds(pl.multiple_of(node * width, width), width)
        shared_scr[...] = dot(ordered_scr[...], x_scr[:, columns], 0, 0).astype(BF16)
        write(shared_scr, shared_ref)
        for copy in copies:
            copy.wait()

    return pl.pallas_call(
        kernel,
        out_shape=(
            jax.ShapeDtypeStruct((experts, units, features), BF16),
            jax.ShapeDtypeStruct((experts, slot_total, units), BF16),
            jax.ShapeDtypeStruct((shared_units, width), BF16),
        ),
        in_specs=[SMEM] + [ANY] * 5 + [VMEM] * 6,
        out_specs=[ANY] * 3,
        scratch_shapes=[
            pltpu.VMEM((2 * tokens, features), BF16),
            pltpu.VMEM((experts, units, 2 * tokens), BF16),
            pltpu.VMEM((experts, units, 2 * tokens), BF16),
            pltpu.VMEM((4 * node_tokens, shared_units), BF16),
            pltpu.VMEM((4 * node_tokens, shared_units), BF16),
            pltpu.VMEM((experts * parts, step, features), BF16),
            pltpu.VMEM((experts, slot_total, units), BF16),
            pltpu.VMEM((shared_units, width), BF16),
            pltpu.SemaphoreType.DMA((6,)),
            pltpu.SemaphoreType.DMA((experts * parts + experts + 1,)),
        ],
        compiler_params=pltpu.CompilerParams(vmem_limit_bytes=LAST_MIB * MIB),
        cost_estimate=pl.CostEstimate(flops=8 * 10**9, bytes_accessed=10**7, transcendentals=0),
        name="last",
    )(where, rows, first[1], second[1], first[2], second[2], first[3], second[3], *shared)


def shared_back_call(counts, where, weights, blocks, down):
    units, features = down.shape
    here = blocks[0].shape[0]
    tokens = here * counts[1]

    def kernel(where_ref, *refs):
        blocks, (weights_ref, down_ref, out_ref, near_scr) = refs[:-4], refs[-4:]
        node, local = where_ref[0], where_ref[1]
        for block, number in zip(blocks, block_numbers(node, local, *counts)[::2]):

            @pl.when(number // counts[1] == node)
            def _(block=block, number=number):
                to = pl.ds(pl.multiple_of(number % counts[1] * here, here), here)
                near_scr[to, :] = block[:, :features]

        back = dot(down_ref[...], near_scr[...], 1, 1) * weights_ref[1:2, :tokens]
        out_ref[...] = back.T.astype(BF16)

    return pl.pallas_call(
        kernel,
        out_shape=jax.ShapeDtypeStruct((tokens, units), BF16),
        in_specs=[SMEM] + [VMEM] * (len(blocks) + 2),
        out_specs=VMEM,
        scratch_shapes=[pltpu.VMEM((tokens, features), BF16)],
        compiler_params=pltpu.CompilerParams(vmem_limit_bytes=12 * MIB),
        cost_estimate=pl.CostEstimate(flops=SHARED_FLOPS, bytes_accessed=10**6, transcendentals=0),
        name="shared_back",
    )(where, *blocks, weights, down)


def gates_call(counts, parts, ids):
    experts = parts.shape[1]

    def kernel(ids_ref, parts_ref, out_ref):
        d_gate = jnp.zeros(out_ref.shape, F32)
        for node in range(counts[0]):
            total = parts_ref[node * counts[1]]
            for local in range(1, counts[1]):
                total = total + parts_ref[node * counts[1] + local]
            for e in range(experts):
                d_gate = d_gate + jnp.where(ids_ref[...] == node * experts + e, total[e : e + 1], 0.0)
        out_ref[...] = d_gate

    return pl.pallas_call(
        kernel,
        out_shape=jax.ShapeDtypeStruct(ids.shape, F32),
        in_specs=[VMEM] * 2,
        out_specs=VMEM,
        compiler_params=pltpu.CompilerParams(vmem_limit_bytes=4 * MIB),
        cost_estimate=LITTLE,
        name="gates",
    )(ids, parts)


def exchanged(a):
    return lax.all_to_all(a, AXES, split_axis=0, concat_axis=0, tiled=True)


def wide_body(
    out_grad,
    lengths,
    gate_weights,
    expert_ids,
    hidden_routed,
    down_routed,
    hidden_shared,
    down_shared,
):
    node_count = lax.axis_size("node")
    local_count = lax.axis_size("local")
    device_count = node_count * local_count
    here, features = out_grad.shape
    choices = expert_ids.shape[1]
    experts, slot_total, units = hidden_routed.shape
    capacity = slot_total // device_count
    node = lax.axis_index("node")
    pad = jnp.zeros((here, 128 - 2 * choices), BF16)
    packed = jnp.concatenate([out_grad, gate_weights, expert_ids.astype(BF16), pad], axis=1)
    rows = lax.all_gather(packed, AXES, axis=0, tiled=True)
    token_total = device_count * here
    ends = jnp.cumsum(lengths)
    places = jnp.arange(token_total, dtype=jnp.int32)
    inside = (places[:, None] >= (ends - lengths)[None, :]) & (places[:, None] < ends[None, :])
    weight = MEAN_LENGTH / jnp.sum(jnp.where(inside, lengths[None, :], 0), axis=1).astype(F32)
    x = rows[:, :features]
    gates = rows[:, features : features + choices].astype(F32)
    ids = rows[:, features + choices : features + 2 * choices].astype(jnp.int32)
    d_hidden, d_down, sums = [], [], []
    for e in range(experts):
        named = ids == node * experts + e
        hit = jnp.any(named, axis=1)
        gate = jnp.sum(jnp.where(named, gates, 0.0), axis=1)
        hits = hit.astype(jnp.int32).reshape(device_count, here)
        rank = (jnp.cumsum(hits, axis=1) - hits).reshape(-1)
        cell = places // here * capacity + rank
        cell = jnp.where(hit & (rank < capacity), cell, -1)
        placing = jnp.arange(slot_total, dtype=jnp.int32)[:, None] == cell[None, :]
        placing = placing.astype(BF16)
        hidden = dot(hidden_routed[e], placing, 0, 0)
        back = dot(down_routed[e], x, 1, 1) * weight[None, :]
        sums.append(jnp.sum(hidden * back, axis=0))
        gated = placing * gate.astype(BF16)[None, :]
        d_hidden.append(dot(gated, back.astype(BF16), 1, 1).astype(BF16))
        scaled = (hidden * (gate * weight)[None, :]).astype(BF16)
        d_down.append(dot(scaled, x, 1, 0).astype(BF16))
    slot_grad = jnp.stack(sums).reshape(experts, device_count, here)
    where = jnp.stack([node, lax.axis_index("local")]).astype(jnp.int32)
    d_gate = gates_call((node_count, local_count), exchanged(jnp.swapaxes(slot_grad, 0, 1)), expert_ids.T).T
    near_total = local_count * here
    near = lax.dynamic_slice_in_dim(x, node * near_total, near_total, 0)
    near_weight = lax.dynamic_slice_in_dim(weight, node * near_total, near_total, 0)
    shared_back = dot(near, down_shared, 1, 1)
    d_hidden_shared = (shared_back * near_weight[:, None]).astype(BF16)
    columns = features // node_count
    mine = lax.dynamic_slice_in_dim(x, node * columns, columns, 1)
    shared = lax.all_gather(hidden_shared, "node", axis=0, tiled=True)
    shared = (shared.astype(F32) * weight[:, None]).astype(BF16)
    d_down_shared = dot(shared, mine, 0, 0).astype(BF16)
    return (jnp.stack(d_hidden), jnp.stack(d_down), d_gate, d_hidden_shared, d_down_shared)


def body(
    out_grad,
    lengths,
    gate_weights,
    expert_ids,
    hidden_routed,
    down_routed,
    hidden_shared,
    down_shared,
):
    counts = lax.axis_size("node"), lax.axis_size("local")
    device_count = counts[0] * counts[1]
    here, features = out_grad.shape
    choices = expert_ids.shape[1]
    slot_total = hidden_routed.shape[1]
    capacity = slot_total // device_count
    where = jnp.stack([lax.axis_index("node"), lax.axis_index("local")]).astype(jnp.int32)
    up, down = ring_shift(*counts, 1), ring_shift(*counts, -1)

    def send(a, pairs):
        return lax.ppermute(a, AXES, pairs)

    def swapped(a):
        return lax.ppermute(a, "node", [(n, n ^ 1) for n in range(counts[0])])

    together = lax.optimization_barrier
    packed, where = together((pack_call(out_grad, gate_weights.T, expert_ids.T), where))
    forth, back, other = [packed], [packed], [swapped(packed)]
    weights, shared, turned = weights_call(counts, lengths, where, hidden_shared, hidden_routed)
    for step in range(3):
        forth.append(send(forth[-1], up))
        back.append(send(back[-1], down))
        other += [swapped(forth[-1]), swapped(back[-1])]
        if step == 0:
            forth[-1], weights, shared, turned = together((forth[-1], weights, shared, turned))
            shared = [shared, swapped(shared)]
        if step == 1:
            forth[-1], shared = together((forth[-1], shared))
    own = [packed, forth[1], back[1], forth[2], back[2], forth[3], back[3]]
    early = [block for pair in zip(own[:4], other[:4]) for block in pair]
    first = half_call(
        counts, capacity, choices, 0, where, weights, early, down_routed, turned, None, None
    )
    rows, *first = first
    forth[3], first[3] = together((forth[3], first[3]))
    own[-2:] = forth[3], back[3]
    split = features * 5 // 8 // 128 * 128
    left, right = send(forth[3][:, :split], up), send(back[3][:, split:], down)
    d_hidden_shared = shared_back_call(counts, where, weights, own, down_shared)
    left, right, shared, d_hidden_shared = together((left, right, shared, d_hidden_shared))
    own.append(jnp.concatenate([left, right], axis=1))
    other.append(swapped(own[-1]))
    shared.append(lax.ppermute(shared[0], "node", [(n, n ^ 2) for n in range(counts[0])]))
    late = [block for pair in zip(own[4:], other[4:]) for block in pair]
    second = half_call(
        counts, capacity, choices, len(early), where, weights, late, down_routed, turned, rows, first[3]
    )
    rows, *second = second
    second[3], shared[2] = together((second[3], shared[2]))
    shared.append(swapped(shared[2]))
    parts = exchanged(second[3])
    d_down, d_hidden_routed, d_down_shared = last_call(
        counts, slot_total, where, rows, (None, *first[:3]), (None, *second[:3]), shared
    )
    parts, d_down_shared = together((parts, d_down_shared))
    d_gate = gates_call(counts, parts, expert_ids.T).T
    return (d_hidden_routed, d_down, d_gate, d_hidden_shared, d_down_shared)


def solution(mesh):
    placed = (
        P(("groups", "node", "local"), None),
        P("groups"),
        P(("groups", "node", "local"), None),
        P(("groups", "node", "local"), None),
        P("node", "groups", "local"),
        P("node", "local", None),
        P(("groups", "node"), "local"),
        P("local", None),
    )
    small = mesh.shape["node"] == 4 and mesh.shape["local"] == 4
    return jax.shard_map(
        body if small else wide_body,
        mesh=mesh,
        in_specs=placed,
        out_specs=(
            P("node", "groups", "local"),
            P(("groups", "node"), "local", None),
            P(("groups", "node", "local"), None),
            P(("groups", "node"), "local"),
            P(("groups", "local"), "node"),
        ),
        check_vma=False,
    )
```
